128 devices in a mesh: bag: 8 (over x, core), sp: 16 (over z, y).
Axes of the slice: x: 4, y: 4, z: 4, core: 2. Of those that a mesh axis runs over, the one named last changes fastest.
Arguments:
- tokens: bfloat16 [32768, 1152], P(('bag', 'sp')), may hold values from -8 to 8
- row_seq: int32 [32768], P(('bag', 'sp')), may hold values from 0 to 7, as said below
- modulation: float32 [8, 6, 1152], replicated, may hold values from -4 to 4
- w_qkv: bfloat16 [1152, 3456], replicated, may hold values from -1 to 1
- w_out: bfloat16 [1152, 1152], replicated, may hold values from -0.1875 to 0.1875
- w_fc1: bfloat16 [1152, 2304], replicated, may hold values from -0.1875 to 0.1875
- w_fc2: bfloat16 [2304, 1152], replicated, may hold values from -0.125 to 0.125
Outputs:
- output: bfloat16 [32768, 1152], P(('bag', 'sp'))
The draws below stay inside these ranges and needn't reach their ends.
Inputs may be any that keep to these rules, and one draw needn't show every extreme that they name: `row_seq`: rows 2m and 2m + 1 belong to the same sequence. Sequence s lies in bag s. Of one device's 256 rows at most 40 lie in any one bag, and on every device exactly 40 lie in one bag. Every sequence has rows.
All inputs are finite; a program needn't handle non-finite values.
Results may differ from the reference program's by a relative error of at most 0.0095.
Values may be sent and summed in bfloat16 or wider, within the bound.
A program may use at most 128 MiB of HBM per device.

```python
import math
import jax
import jax.numpy as jnp
from jax import lax

D = 1152
H = 16
HD = 72
FF = 2304
SEQ_BAG = 1
ROWS_DEV = 256
BAG_SLOTS = 5120
SEQS = 8
TOKENS = 32768
N_BAG = 8
N_SP = 16


def draw_row_seq(key, part):
    base_key = jax.random.fold_in(key, 5)
    key_list = jax.random.split(base_key, 6)
    device_total = N_BAG * N_SP
    pair_count = ROWS_DEV // 2
    mean_pairs = pair_count // N_BAG
    extra = mean_pairs // 4
    bag_perms = jax.vmap(lambda one_key: jax.random.permutation(one_key, N_BAG))(jax.random.split(key_list[0], device_total))
    shifted = jax.random.randint(key_list[1], (device_total,), 0, max(extra, 1))
    bag_ids = jnp.arange(N_BAG, dtype=jnp.int32)

    def one_hot(column):
        return (bag_perms[:, column][:, None] == bag_ids[None, :]).astype(jnp.int32)
    counts = mean_pairs + extra * (one_hot(0) - one_hot(1)) + shifted[:, None] * (one_hot(2) - one_hot(3))
    ends = jnp.cumsum(counts, axis=1)
    pair_ids = jnp.arange(pair_count, dtype=jnp.int32)
    bag_of_pair = jnp.sum((pair_ids[None, :, None] >= ends[:, None, :]).astype(jnp.int32), axis=-1)
    pair_perms = jax.vmap(lambda one_key: jax.random.permutation(one_key, pair_count))(jax.random.split(key_list[2], device_total))
    bag_of_pair = jnp.take_along_axis(bag_of_pair, pair_perms, axis=1)
    first_pick = jax.random.randint(key_list[3], (device_total, pair_count), 0, SEQ_BAG)
    second_pick = jax.random.randint(key_list[4], (device_total, pair_count), 0, SEQ_BAG)
    within = jnp.minimum(first_pick, second_pick)
    seq_perms = jax.vmap(lambda one_key: jax.random.permutation(one_key, SEQ_BAG))(jax.random.split(key_list[5], N_BAG))
    local_seq = seq_perms[bag_of_pair, within]
    seq_ids = (bag_of_pair * SEQ_BAG + local_seq).astype(jnp.int32)
    return jnp.repeat(seq_ids, 2, axis=1).reshape(TOKENS).astype(jnp.int32)


def draw_tokens(key, part):
    base = jnp.clip(jax.random.normal(jax.random.fold_in(key, 11), (TOKENS, D), jnp.float32), -6.0, 6.0)
    return base.astype(jnp.bfloat16)


def draw_modulation(key, part):
    table = 0.5 * jnp.clip(jax.random.normal(jax.random.fold_in(key, 21), (SEQS, 6, D), jnp.float32), -6.0, 6.0)
    return table


def draw_w_qkv(key, part):
    matrix = jnp.clip(jax.random.normal(jax.random.fold_in(key, 31), (D, 3, D), jnp.float32), -6.0, 6.0) / jnp.sqrt(jnp.float32(D))
    return matrix.reshape(D, 3 * D).astype(jnp.bfloat16)


def scatter_about(key, dims, scale, limit, kind=jnp.bfloat16):
    result = scale * jax.random.normal(key, dims, jnp.float32)
    return jnp.clip(result, min=-limit, max=limit).astype(kind)


def setup_inputs(seed: int = 0) -> dict:
    seeds = jax.random.split(jax.random.key(seed), 8)
    return {
        "tokens": draw_tokens(jax.random.fold_in(seeds[7], 71), 0),
        "row_seq": draw_row_seq(jax.random.fold_in(seeds[7], 71), 0),
        "modulation": draw_modulation(jax.random.fold_in(seeds[7], 71), 0),
        "w_qkv": draw_w_qkv(jax.random.fold_in(seeds[7], 71), 0),
        "w_out": scatter_about(seeds[4], (D, D), D ** -0.5, 0.1875),
        "w_fc1": scatter_about(seeds[5], (D, FF), D ** -0.5, 0.1875),
        "w_fc2": scatter_about(seeds[6], (FF, D), FF ** -0.5, 0.125),
    }


EPS = 1e-06

def layer_norm(values):
    center = values - lax.optimization_barrier(jnp.mean(values, axis=-1, keepdims=True))
    spread = lax.optimization_barrier(jnp.mean(center * center, axis=-1, keepdims=True))
    return center * lax.rsqrt(spread + EPS)

def reference(tokens, row_seq, modulation, w_qkv, w_out, w_fc1, w_fc2):
    total_rows = tokens.shape[0]

    def per_row(column):
        return jnp.take(modulation[:, column, :], row_seq, axis=0)
    normed1 = (layer_norm(tokens.astype(jnp.float32)) * (1.0 + per_row(1)) + per_row(0)).astype(jnp.bfloat16)
    qkv = jnp.dot(normed1, w_qkv, preferred_element_type=jnp.float32).astype(jnp.bfloat16)
    order = jnp.argsort(row_seq, stable=True).astype(jnp.int32)
    seq_sorted = jnp.take(row_seq, order)
    qkv_sorted = jnp.take(qkv, order, axis=0).reshape(total_rows, 3, H, HD)
    member = (row_seq[:, None] == jnp.arange(SEQS, dtype=jnp.int32)[None, :]).astype(jnp.int32)
    counts = lax.optimization_barrier(jnp.sum(member, axis=0))
    starts = (jnp.cumsum(counts) - counts).astype(jnp.int32)
    block_size = math.gcd(total_rows, 512)
    window = min(total_rows, 2 * BAG_SLOTS + block_size)
    score_scale = 1.0 / math.sqrt(HD)

    def one_block(block_index):
        first_row = (block_index * block_size).astype(jnp.int32)
        query_part = lax.dynamic_slice_in_dim(qkv_sorted, first_row, block_size, 0)
        query_seq = lax.dynamic_slice_in_dim(seq_sorted, first_row, block_size, 0)
        key_start = jnp.minimum(starts[query_seq[0]], total_rows - window).astype(jnp.int32)
        key_part = lax.dynamic_slice_in_dim(qkv_sorted, key_start, window, 0)
        key_seq = lax.dynamic_slice_in_dim(seq_sorted, key_start, window, 0)
        queries = query_part[:, 0].astype(jnp.float32)
        key_rows = key_part[:, 1].astype(jnp.float32)
        values = key_part[:, 2].astype(jnp.float32)
        scores = jnp.einsum('qhd,khd->hqk', queries, key_rows) * score_scale
        allowed = query_seq[:, None] == key_seq[None, :]
        scores = jnp.where(allowed[None], scores, -jnp.inf)
        row_max = lax.optimization_barrier(jnp.max(scores, axis=-1, keepdims=True))
        raised = jnp.exp(scores - row_max)
        denominator = lax.optimization_barrier(jnp.sum(raised, axis=-1))
        probs = raised.astype(jnp.bfloat16).astype(jnp.float32)
        mixed_rows = jnp.einsum('hqk,khd->qhd', probs, values)
        mixed_rows = mixed_rows / jnp.transpose(denominator)[:, :, None]
        return mixed_rows.astype(jnp.bfloat16).reshape(block_size, D)
    attended_sorted = lax.map(one_block, jnp.arange(total_rows // block_size, dtype=jnp.int32)).reshape(total_rows, D)
    attended = jnp.zeros((total_rows, D), jnp.bfloat16).at[order].set(attended_sorted)
    branch = jnp.dot(attended, w_out, preferred_element_type=jnp.float32)
    hidden = (tokens.astype(jnp.float32) + per_row(2) * branch).astype(jnp.bfloat16)
    normed2 = (layer_norm(hidden.astype(jnp.float32)) * (1.0 + per_row(4)) + per_row(3)).astype(jnp.bfloat16)
    active = jax.nn.gelu(jnp.dot(normed2, w_fc1, preferred_element_type=jnp.float32), approximate=True).astype(jnp.bfloat16)
    return (hidden.astype(jnp.float32) + per_row(5) * jnp.dot(active, w_fc2, preferred_element_type=jnp.float32)).astype(jnp.bfloat16)
```

```python
import functools
import math

import jax
import jax.numpy as jnp
from jax import lax
from jax.experimental import pallas as pl
from jax.experimental.pallas import tpu as pltpu
from jax.sharding import PartitionSpec as P

MESH = pl.DeviceIdType.MESH
D = 1152
H = 16
HD = 72
FF = 2304
BAGS = 8
CAP = 40
ROWS = 256
SLOTS = BAGS * CAP
DEVS = 128
GROUPS = 4
PER = DEVS // GROUPS
GROWS = PER * CAP
KEYS = DEVS * CAP
QT = 1280
QHEAD = 55
EPS = 1e-6
BIG = 1e30
F32 = jnp.float32
BF16 = jnp.bfloat16


def peer(g, i, sign):
    bag, sp = lax.axis_index("bag"), lax.axis_index("sp")
    x, c, z, y = bag // 2, lax.rem(bag, 2), sp // 4, lax.rem(sp, 4)
    dc, dx, dy = lax.rem(i, 2), lax.rem(i // 2, 4), i // 8
    dz = lax.rem(g + 8 - dx - dy, 4)
    if sign < 0:
        dc, dx, dy, dz = 2 - dc, 4 - dx, 4 - dy, 4 - dz
    return (
        lax.rem(x + dx, 4) * 2 + lax.rem(c + dc, 2),
        lax.rem(z + dz, 4) * 4 + lax.rem(y + dy, 4),
    )


def norm(values):
    center = values - jnp.mean(values, axis=-1, keepdims=True)
    spread = jnp.mean(center * center, axis=-1, keepdims=True)
    return center * lax.rsqrt(spread + EPS)


def two_mods(mod_ref, r, which):
    return jnp.concatenate(
        [
            jnp.broadcast_to(mod_ref[2 * r, which : which + 1, :], (CAP, D)),
            jnp.broadcast_to(mod_ref[2 * r + 1, which : which + 1, :], (CAP, D)),
        ],
        axis=0,
    )


def kernel(
    tok_ref, seq_ref, mod_ref, wqkv_hbm, wout_hbm, wfc1_hbm, wfc2_hbm, out_ref,
    wbig, wfc2, send, recv, kbuf, vbuf, qbuf, acc_s, max_s, wide, xs, norms, att, act, place,
    bias_s, osend, orecv, w_sem, ssem, rsem, ssem2, rsem2,
):
    bag, sp = lax.axis_index("bag"), lax.axis_index("sp")
    me = bag * H + sp
    barrier = pltpu.get_barrier_semaphore()

    copy_qkv = pltpu.make_async_copy(wqkv_hbm, wbig, w_sem.at[0])
    copy_qkv.start()
    copy_fc2 = pltpu.make_async_copy(wfc2_hbm, wfc2, w_sem.at[1])
    copy_fc2.start()

    def greet(n, carry):
        b, s = peer(n // PER, lax.rem(n, PER), 1)
        pl.semaphore_signal(barrier, inc=1, device_id=(b, s), device_id_type=MESH)
        return carry

    lax.fori_loop(1, DEVS, greet, 0)

    seq = seq_ref[...]
    member = (lax.broadcasted_iota(jnp.int32, (BAGS, ROWS), 0) == seq).astype(F32)
    earlier = (
        lax.broadcasted_iota(jnp.int32, (ROWS, ROWS), 0)
        < lax.broadcasted_iota(jnp.int32, (ROWS, ROWS), 1)
    ).astype(BF16)
    before = jnp.dot(member.astype(BF16), earlier, preferred_element_type=F32)
    rank = jnp.sum(member * before, axis=0, keepdims=True)
    position = seq.astype(F32) * CAP + rank
    one_hot = (
        lax.broadcasted_iota(jnp.int32, (SLOTS, ROWS), 0).astype(F32) == position
    ).astype(F32)
    bias_s[...] = jnp.broadcast_to(
        (jnp.sum(one_hot, axis=1, keepdims=True) - 1.0) * BIG, (SLOTS, 128)
    )
    place[...] = one_hot.astype(BF16)
    xs[...] = jnp.dot(place[...], tok_ref[...], preferred_element_type=F32)

    @pl.loop(0, BAGS // 2)
    def _(r):
        rows = pl.ds(pl.multiple_of(r * 2 * CAP, 2 * CAP), 2 * CAP)
        norms[rows, :] = (
            norm(xs[rows, :]) * (1.0 + two_mods(mod_ref, r, 1)) + two_mods(mod_ref, r, 0)
        ).astype(BF16)

    copy_qkv.wait()
    scale = math.log2(math.e) / math.sqrt(HD)
    for part in range(3):
        cols = pl.ds(part * D, D)
        wide[:, cols] = jnp.dot(norms[...], wbig[:, cols], preferred_element_type=F32) * (
            scale if part == 0 else 1.0
        )
    copy_out = pltpu.make_async_copy(wout_hbm, wbig.at[:, pl.ds(0, D)], w_sem.at[2])
    copy_out.start()
    copy_fc1 = pltpu.make_async_copy(wfc1_hbm, wbig.at[:, pl.ds(D, FF)], w_sem.at[3])
    copy_fc1.start()

    lane = lax.broadcasted_iota(jnp.int32, (CAP, 128), 1)

    @pl.loop(0, BAGS)
    def _(r):
        rows = pl.ds(pl.multiple_of(r * CAP, 8), CAP)

        def piece(column, width, target):
            first, off = column // 128 * 128, column % 128
            shift = (target - off) % 128
            main = wide[rows, first : first + 128]
            if shift:
                main = pltpu.roll(main, shift, 1)
            if off + width > 128:
                rest = wide[rows, first + 128 : first + 256]
                if shift:
                    rest = pltpu.roll(rest, shift, 1)
                main = jnp.where(lane < target + 128 - off, main, rest)
            return main

        bias = bias_s[rows, :]
        for h in range(H):
            keys = jnp.where(lane < HD, piece(D + HD * h, HD, 0), piece(HD * h, QHEAD, HD + 1))
            keys = jnp.where(lane == HD, bias, keys)
            values = jnp.where(
                lane < HD,
                piece(2 * D + HD * h, HD, 0),
                piece(HD * h + QHEAD, HD - QHEAD, HD + 1),
            )
            values = jnp.where(lane == HD, 1.0, values)
            values = jnp.where(lane < HD + 1 + HD - QHEAD, values, 0.0)
            send[r * H + h] = jnp.concatenate([keys, values], axis=0).astype(BF16)

    pl.semaphore_wait(barrier, DEVS - 1)
    for g in range(GROUPS):

        def push(i, carry, g=g):
            b, s = peer(g, i, 1)
            pltpu.make_async_remote_copy(
                src_ref=send.at[b * H + s],
                dst_ref=recv.at[g * PER + i],
                send_sem=ssem.at[g],
                recv_sem=rsem.at[g],
                device_id=(b, s),
                device_id_type=MESH,
            ).start()
            return carry

        lax.fori_loop(1 if g == 0 else 0, PER, push, 0)
    recv[0] = send[me]

    def group_copy(g):
        first = g * PER + (1 if g == 0 else 0)
        block = recv.at[pl.ds(first, (g + 1) * PER - first)]
        return pltpu.make_async_remote_copy(
            src_ref=block,
            dst_ref=block,
            send_sem=ssem.at[g],
            recv_sem=rsem.at[g],
            device_id=(bag, lax.rem(sp + 1, H)),
            device_id_type=MESH,
        )

    lane2 = lax.broadcasted_iota(jnp.int32, (2 * CAP, 128), 1)

    def unpack(g):
        @pl.loop(g * PER // 2, (g + 1) * PER // 2)
        def _(n):
            one = recv[2 * n].astype(F32)
            two = recv[2 * n + 1].astype(F32)
            keys = jnp.concatenate([one[:CAP], two[:CAP]], axis=0)
            values = jnp.concatenate([one[CAP:], two[CAP:]], axis=0)
            query = jnp.where(
                lane2 < QHEAD,
                pltpu.roll(keys, 127 - HD, 1),
                pltpu.roll(values, (QHEAD - HD - 1) % 128, 1),
            )
            query = jnp.where(lane2 < HD, query, jnp.where(lane2 == HD, 1.0, 0.0))
            rows = pl.ds(pl.multiple_of(n * 2 * CAP, 2 * CAP), 2 * CAP)
            kbuf[rows, :] = keys.astype(BF16)
            vbuf[rows, :] = values.astype(BF16)
            qbuf[rows, :] = query.astype(BF16)

    def attend(rows, key_group):
        keys = pl.ds(pl.multiple_of(key_group * GROWS, GROWS), GROWS)
        scores = lax.dot_general(
            qbuf[rows, :], kbuf[keys, :], (((1,), (1,)), ((), ())), preferred_element_type=F32
        )
        old = max_s[rows, :]
        new = jnp.maximum(old, jnp.max(scores, axis=1, keepdims=True))
        probs = jnp.exp2(scores - new).astype(BF16)
        acc_s[rows, :] = acc_s[rows, :] * jnp.exp2(old - new) + jnp.dot(
            probs, vbuf[keys, :], preferred_element_type=F32
        )
        max_s[rows, :] = new

    lane32 = lax.broadcasted_iota(jnp.int32, (8, 128), 1)

    def give_back(tile):
        def one_source(k, carry):
            rows = pl.ds(pl.multiple_of(k * CAP, 8), CAP)
            mixed = acc_s[rows, :]
            mixed = mixed / mixed[:, HD : HD + 1]
            tail = mixed[32:40]
            packed = jnp.concatenate(
                [
                    jnp.where(lane32 < HD, mixed[0:8], pltpu.roll(tail, HD, 1)),
                    jnp.where(lane32 < HD, mixed[8:16], pltpu.roll(tail, 16, 1)),
                    mixed[16:32],
                ],
                axis=0,
            )
            osend[k] = packed.astype(BF16)
            return carry

        def push(k, carry):
            b, s = peer(k // PER, lax.rem(k, PER), -1)
            pltpu.make_async_remote_copy(
                src_ref=osend.at[k],
                dst_ref=orecv.at[me],
                send_sem=ssem2,
                recv_sem=rsem2,
                device_id=(b, s),
                device_id_type=MESH,
            ).start()
            return carry

        per_tile = QT // CAP
        lax.fori_loop(tile * per_tile, (tile + 1) * per_tile, one_source, 0)
        if isinstance(tile, int) and tile == 0:
            lax.fori_loop(1, per_tile, push, 0)
            orecv[me] = osend[0]
        else:
            lax.fori_loop(tile * per_tile, (tile + 1) * per_tile, push, 0)

    tiles = GROWS // QT
    max_s[...] = jnp.full((KEYS, 1), -BIG, F32)
    acc_s[...] = jnp.zeros((KEYS, 128), F32)
    for g in range(GROUPS):
        group_copy(g).wait_recv()
        unpack(g)
        last = g == GROUPS - 1
        for t in range((g + 1) * tiles):
            rows = pl.ds(t * QT, QT)
            if t < g * tiles:
                attend(rows, g)
            else:

                @pl.loop(0, g + 1)
                def _(k, rows=rows):
                    attend(rows, k)

            if last:
                give_back(t)

    def return_copy(buf, lo):
        block = buf.at[pl.ds(lo, DEVS - 1)]
        return pltpu.make_async_remote_copy(
            src_ref=block,
            dst_ref=block,
            send_sem=ssem2,
            recv_sem=rsem2,
            device_id=(bag, lax.rem(sp + 1, H)),
            device_id_type=MESH,
        )

    return_copy(orecv, 0).wait_recv()

    @pl.loop(0, BAGS // 2)
    def _(rp):
        halves = []
        for r in range(2):
            moved = []
            for h in range(H):
                block = orecv[(2 * rp + r) * H + h].astype(F32)
                tail = jnp.where(
                    lane32 < 128 - HD,
                    pltpu.roll(block[0:8], 128 - HD, 1),
                    pltpu.roll(block[8:16], 112, 1),
                )
                whole = jnp.concatenate([block, tail], axis=0)
                shift = HD * h % 128
                moved.append(pltpu.roll(whole, shift, 1) if shift else whole)
            columns = []
            for j in range(D // 128):
                first = 128 * j // HD
                column = moved[first]
                for h in range(first + 1, H):
                    if HD * h >= 128 * (j + 1):
                        break
                    column = jnp.where(lane < HD * h - 128 * j, column, moved[h])
                columns.append(column)
            halves.append(columns)
        rows = pl.ds(pl.multiple_of(rp * 2 * CAP, 2 * CAP), 2 * CAP)
        for j in range(D // 128):
            att[rows, 128 * j : 128 * j + 128] = jnp.concatenate(
                [halves[0][j], halves[1][j]], axis=0
            ).astype(BF16)

    copy_out.wait()
    wide[:, 0:D] = jnp.dot(att[...], wbig[:, 0:D], preferred_element_type=F32)

    @pl.loop(0, BAGS // 2)
    def _(r):
        rows = pl.ds(pl.multiple_of(r * 2 * CAP, 2 * CAP), 2 * CAP)
        hidden = (xs[rows, :] + two_mods(mod_ref, r, 2) * wide[rows, 0:D]).astype(BF16).astype(F32)
        xs[rows, :] = hidden
        norms[rows, :] = (
            norm(hidden) * (1.0 + two_mods(mod_ref, r, 4)) + two_mods(mod_ref, r, 3)
        ).astype(BF16)

    copy_fc1.wait()
    for part in range(2):
        inner = jnp.dot(
            norms[...], wbig[:, D * (part + 1) : D * (part + 2)], preferred_element_type=F32
        )
        act[:, D * part : D * (part + 1)] = jax.nn.gelu(inner, approximate=True).astype(BF16)
    copy_fc2.wait()
    wide[:, 0:D] = jnp.dot(act[...], wfc2[...], preferred_element_type=F32)

    @pl.loop(0, BAGS // 2)
    def _(r):
        rows = pl.ds(pl.multiple_of(r * 2 * CAP, 2 * CAP), 2 * CAP)
        att[rows, :] = (xs[rows, :] + two_mods(mod_ref, r, 5) * wide[rows, 0:D]).astype(BF16)

    out_ref[...] = lax.dot_general(
        place[...], att[...], (((0,), (0,)), ((), ())), preferred_element_type=F32
    ).astype(BF16)

    for g in range(GROUPS):
        group_copy(g).wait_send()
    return_copy(osend, 1).wait_send()


def shards(tokens, row_seq, modulation, w_qkv, w_out, w_fc1, w_fc2):
    vmem = pl.BlockSpec(memory_space=pltpu.VMEM)
    anywhere = pl.BlockSpec(memory_space=pl.ANY)
    return pl.pallas_call(
        kernel,
        out_shape=jax.ShapeDtypeStruct((ROWS, D), BF16),
        in_specs=[vmem, vmem, vmem, anywhere, anywhere, anywhere, anywhere],
        out_specs=vmem,
        scratch_shapes=[
            pltpu.VMEM((D, 3 * D), BF16),
            pltpu.VMEM((FF, D), BF16),
            pltpu.VMEM((DEVS, 2 * CAP, 128), BF16),
            pltpu.VMEM((DEVS, 2 * CAP, 128), BF16),
            pltpu.VMEM((KEYS, 128), BF16),
            pltpu.VMEM((KEYS, 128), BF16),
            pltpu.VMEM((KEYS, 128), BF16),
            pltpu.VMEM((KEYS, 128), F32),
            pltpu.VMEM((KEYS, 1), F32),
            pltpu.VMEM((SLOTS, 3 * D), F32),
            pltpu.VMEM((SLOTS, D), F32),
            pltpu.VMEM((SLOTS, D), BF16),
            pltpu.VMEM((SLOTS, D), BF16),
            pltpu.VMEM((SLOTS, FF), BF16),
            pltpu.VMEM((SLOTS, ROWS), BF16),
            pltpu.VMEM((SLOTS, 128), F32),
            pltpu.VMEM((DEVS, 32, 128), BF16),
            pltpu.VMEM((DEVS, 32, 128), BF16),
            pltpu.SemaphoreType.DMA((4,)),
            pltpu.SemaphoreType.DMA((GROUPS,)),
            pltpu.SemaphoreType.DMA((GROUPS,)),
            pltpu.SemaphoreType.DMA,
            pltpu.SemaphoreType.DMA,
        ],
        compiler_params=pltpu.CompilerParams(
            collective_id=0, has_side_effects=True, vmem_limit_bytes=62 * 2**20
        ),
    )(tokens, row_seq.reshape(1, ROWS), modulation, w_qkv, w_out, w_fc1, w_fc2)


def solution(mesh):
    placed = (P(("bag", "sp"), None), P(("bag", "sp")), P(), P(), P(), P(), P())
    return jax.shard_map(
        shards, mesh=mesh, in_specs=placed, out_specs=P(("bag", "sp"), None), check_vma=False
    )
```

```python
import functools
import math

import jax
import jax.numpy as jnp
from jax import lax
from jax.experimental import pallas as pl
from jax.experimental.pallas import tpu as pltpu
from jax.sharding import PartitionSpec as P

MESH = pl.DeviceIdType.MESH
D = 1152
H = 16
HD = 72
FF = 2304
BAGS = 8
CAP = 40
ROWS = 256
SLOTS = BAGS * CAP
DEVS = 128
GROUPS = 4
PER = DEVS // GROUPS
GROWS = PER * CAP
KEYS = DEVS * CAP
QT = 1280
WIDE = 80
LIMIT = 90.0
AHEAD = 2
QHEAD = 55
QLANE = 96
EPS = 1e-6
BIG = 1e30
F32 = jnp.float32
BF16 = jnp.bfloat16


def peers(g, dy, sign):
    bag, sp = lax.axis_index("bag"), lax.axis_index("sp")
    x, c, z, y = bag // 2, lax.rem(bag, 2), sp // 4, lax.rem(sp, 4)
    row = lax.rem(y + 4 + sign * dy, 4)
    cores = [c, 1 - c]
    found = []
    for dx in range(4):
        bags = lax.rem(x + 4 + sign * dx, 4) * 2
        heads = lax.rem(z + 8 + sign * (g - dx - dy), 4) * 4 + row
        found += [(bags + cores[0], heads), (bags + cores[1], heads)]
    return found


def each_peer(g, sign, act, rows=(0, 4)):
    def one_row(dy, carry):
        for n, device in enumerate(peers(g, dy, sign)):
            act(dy * 8 + n, device)
        return carry

    low, high = rows
    if g == 0 and low == 0:
        for n, device in enumerate(peers(g, 0, sign)):
            if n:
                act(n, device)
        low = 1
    lax.fori_loop(low, high, one_row, 0)


def norm(values):
    center = values - jnp.mean(values, axis=-1, keepdims=True)
    spread = jnp.mean(center * center, axis=-1, keepdims=True)
    return center * lax.rsqrt(spread + EPS)


def two_mods(mod_ref, r, which):
    return jnp.concatenate(
        [
            jnp.broadcast_to(mod_ref[which, pl.ds(2 * r, 1), :], (CAP, D)),
            jnp.broadcast_to(mod_ref[which, pl.ds(2 * r + 1, 1), :], (CAP, D)),
        ],
        axis=0,
    )


def kernel(
    tok_ref, seq_ref, mod_ref, wqkv_hbm, wout_hbm, wfc1_hbm, wfc2_hbm, out_ref, bound_ref,
    wbig, wfc2, send, recv, kbuf, vbuf, qbuf, acc_s, stage, peak, wide, xs, norms, att, act, place,
    bias_s, osend, orecv, w_sem, ssem, rsem, ssem2, rsem2,
):
    bag, sp = lax.axis_index("bag"), lax.axis_index("sp")
    me = bag * H + sp
    barrier = pltpu.get_barrier_semaphore()

    copy_qkv = pltpu.make_async_copy(wqkv_hbm, wbig, w_sem.at[0])
    copy_qkv.start()
    copy_fc2 = pltpu.make_async_copy(wfc2_hbm, wfc2, w_sem.at[1])
    copy_fc2.start()

    for g in range(GROUPS):
        each_peer(
            g,
            1,
            lambda i, device: pl.semaphore_signal(
                barrier, inc=1, device_id=device, device_id_type=MESH
            ),
        )

    seq = seq_ref[...]
    member = (lax.broadcasted_iota(jnp.int32, (BAGS, ROWS), 0) == seq).astype(F32)
    earlier = (
        lax.broadcasted_iota(jnp.int32, (ROWS, ROWS), 0)
        < lax.broadcasted_iota(jnp.int32, (ROWS, ROWS), 1)
    ).astype(BF16)
    before = jnp.dot(member.astype(BF16), earlier, preferred_element_type=F32)
    rank = jnp.sum(member * before, axis=0, keepdims=True)
    position = seq.astype(F32) * CAP + rank
    one_hot = (
        lax.broadcasted_iota(jnp.int32, (SLOTS, ROWS), 0).astype(F32) == position
    ).astype(F32)
    bias_s[...] = jnp.broadcast_to(
        (jnp.sum(one_hot, axis=1, keepdims=True) - 1.0) * BIG, (SLOTS, 128)
    )
    place[...] = one_hot.astype(BF16)
    xs[...] = jnp.dot(place[...], tok_ref[...], preferred_element_type=F32)

    @pl.loop(0, BAGS // 2)
    def _(r):
        rows = pl.ds(pl.multiple_of(r * 2 * CAP, 2 * CAP), 2 * CAP)
        norms[rows, :] = (
            norm(xs[rows, :]) * (1.0 + two_mods(mod_ref, r, 1)) + two_mods(mod_ref, r, 0)
        ).astype(BF16)

    copy_qkv.wait()
    scale = math.log2(math.e) / math.sqrt(HD)
    for part in range(3):
        cols = pl.ds(part * D, D)
        wide[:, cols] = jnp.dot(norms[...], wbig[:, cols], preferred_element_type=F32) * (
            scale if part == 0 else 1.0
        )
    feature = lax.broadcasted_iota(jnp.int32, (2 * D, 128), 0)
    first = lax.broadcasted_iota(jnp.int32, (2 * D, 128), 1) * HD
    segment = ((feature >= first) & (feature < first + HD)).astype(BF16)
    squares = wide[:, 0 : 2 * D]
    lengths = 1.02 * jnp.dot(
        (squares * squares).astype(BF16), segment, preferred_element_type=F32
    )
    longest = jnp.max(lengths, axis=0, keepdims=True)
    lane1 = lax.broadcasted_iota(jnp.int32, (1, 128), 1)
    long_q = jnp.max(jnp.where(lane1 < H, longest, 0.0), axis=1, keepdims=True)
    long_k = jnp.max(jnp.where(lane1 >= H, longest, 0.0), axis=1, keepdims=True)
    peak[0:1, :] = jnp.where(lane1 == QLANE, long_q, jnp.where(lane1 == QLANE + 1, long_k, 0.0))
    copy_out = pltpu.make_async_copy(wout_hbm, wbig.at[:, pl.ds(0, D)], w_sem.at[2])
    copy_out.start()
    copy_fc1 = pltpu.make_async_copy(wfc1_hbm, wbig.at[:, pl.ds(D, FF)], w_sem.at[3])
    copy_fc1.start()

    lane = lax.broadcasted_iota(jnp.int32, (CAP, 128), 1)

    @pl.loop(0, BAGS)
    def _(r):
        rows = pl.ds(pl.multiple_of(r * CAP, 8), CAP)

        def piece(column, width, target):
            first, off = column // 128 * 128, column % 128
            shift = (target - off) % 128
            main = wide[rows, first : first + 128]
            if shift:
                main = pltpu.roll(main, shift, 1)
            if off + width > 128:
                rest = wide[rows, first + 128 : first + 256]
                if shift:
                    rest = pltpu.roll(rest, shift, 1)
                main = jnp.where(lane < target + 128 - off, main, rest)
            return main

        bias = bias_s[rows, :]
        lengths = jnp.broadcast_to(peak[0:1, :], (CAP, 128))
        for h in range(H):
            keys = jnp.where(lane < HD, piece(D + HD * h, HD, 0), piece(HD * h, QHEAD, HD + 1))
            keys = jnp.where(lane == HD, bias, keys)
            values = jnp.where(
                lane < HD,
                piece(2 * D + HD * h, HD, 0),
                piece(HD * h + QHEAD, HD - QHEAD, HD + 1),
            )
            values = jnp.where(lane == HD, 1.0, values)
            values = jnp.where(lane < HD + 1 + HD - QHEAD, values, lengths)
            send[r * H + h] = jnp.concatenate([keys, values], axis=0).astype(BF16)

    pl.semaphore_wait(barrier, DEVS - 1)
    def push_group(g):
        def push(i, device):
            pltpu.make_async_remote_copy(
                src_ref=send.at[device[0] * H + device[1]],
                dst_ref=recv.at[g * PER + i],
                send_sem=ssem.at[g],
                recv_sem=rsem.at[g],
                device_id=device,
                device_id_type=MESH,
            ).start()

        each_peer(g, 1, push)

    for g in range(AHEAD):
        push_group(g)
    recv[0] = send[me]

    def group_copy(g):
        first = g * PER + (1 if g == 0 else 0)
        block = recv.at[pl.ds(first, (g + 1) * PER - first)]
        return pltpu.make_async_remote_copy(
            src_ref=block,
            dst_ref=block,
            send_sem=ssem.at[g],
            recv_sem=rsem.at[g],
            device_id=(bag, lax.rem(sp + 1, H)),
            device_id_type=MESH,
        )

    lane2 = lax.broadcasted_iota(jnp.int32, (2 * CAP, 128), 1)

    def unpack(g):
        def two(n, top):
            one = recv[2 * n].astype(F32)
            two = recv[2 * n + 1].astype(F32)
            keys = jnp.concatenate([one[:CAP], two[:CAP]], axis=0)
            values = jnp.concatenate([one[CAP:], two[CAP:]], axis=0)
            query = jnp.where(
                lane2 < QHEAD,
                pltpu.roll(keys, 127 - HD, 1),
                pltpu.roll(values, (QHEAD - HD - 1) % 128, 1),
            )
            query = jnp.where(lane2 < HD, query, jnp.where(lane2 == HD, 1.0, 0.0))
            rows = pl.ds(pl.multiple_of(n * 2 * CAP, 2 * CAP), 2 * CAP)
            kbuf[rows, :] = keys.astype(BF16)
            qbuf[rows, :] = query.astype(BF16)
            near = pl.ds(pl.multiple_of((n - g * PER // 2) * 2 * CAP, 2 * CAP), 2 * CAP)
            stage[near, :] = values
            return jnp.maximum(top, values)

        top = lax.fori_loop(
            g * PER // 2, (g + 1) * PER // 2, two, jnp.zeros((2 * CAP, 128), F32), unroll=2
        )
        bound_ref[...] = jnp.maximum(
            bound_ref[...], jnp.broadcast_to(jnp.max(top, axis=0, keepdims=True), (8, 128))
        )
        vbuf[:, g * GROWS : (g + 1) * GROWS] = stage[...].T[0:WIDE].astype(BF16)

    def attend(first, key_group):
        keys = pl.ds(pl.multiple_of(key_group * GROWS, GROWS), GROWS)
        queries = slice(first, first + QT)
        scores = lax.dot_general(
            kbuf[keys, :], qbuf[queries, :], (((1,), (1,)), ((), ())), preferred_element_type=F32
        )
        acc_s[:, queries] += jnp.dot(
            vbuf[:, keys], jnp.exp2(scores).astype(BF16), preferred_element_type=F32
        )

    lane32 = lax.broadcasted_iota(jnp.int32, (8, 128), 1)

    def give_back(tile):
        mixed = acc_s[:, tile * QT : (tile + 1) * QT]
        mixed = mixed * (1.0 / mixed[HD : HD + 1, :])
        stage[...] = jnp.concatenate([mixed, jnp.zeros((128 - WIDE, QT), F32)], axis=0).T

        def one_source(k, carry):
            mixed = stage[pl.ds(pl.multiple_of((k - tile * PER) * CAP, 8), CAP), :]
            tail = mixed[32:40]
            packed = jnp.concatenate(
                [
                    jnp.where(lane32 < HD, mixed[0:8], pltpu.roll(tail, HD, 1)),
                    jnp.where(lane32 < HD, mixed[8:16], pltpu.roll(tail, 16, 1)),
                    mixed[16:32],
                ],
                axis=0,
            )
            osend[k] = packed.astype(BF16)
            return carry

        def push(i, device):
            pltpu.make_async_remote_copy(
                src_ref=osend.at[tile * PER + i],
                dst_ref=orecv.at[me],
                send_sem=ssem2,
                recv_sem=rsem2,
                device_id=device,
                device_id_type=MESH,
            ).start()

        lax.fori_loop(tile * PER, (tile + 1) * PER, one_source, 0, unroll=8)
        each_peer(tile, -1, push)
        if tile == 0:
            orecv[me] = osend[0]

    tiles = GROWS // QT
    acc_s[...] = jnp.zeros((WIDE, KEYS), F32)
    bound_ref[...] = jnp.zeros((8, 128), F32)
    for g in range(GROUPS):
        group_copy(g).wait_recv()
        if g + AHEAD < GROUPS:
            push_group(g + AHEAD)
        unpack(g)
        last = g == GROUPS - 1
        for t in range((g + 1) * tiles):
            if t < g * tiles:
                attend(t * QT, g)
            else:

                @pl.loop(0, g + 1)
                def _(k, t=t):
                    attend(t * QT, k)

            if last:
                give_back(t)

    def return_copy(buf, lo):
        block = buf.at[pl.ds(lo, DEVS - 1)]
        return pltpu.make_async_remote_copy(
            src_ref=block,
            dst_ref=block,
            send_sem=ssem2,
            recv_sem=rsem2,
            device_id=(bag, lax.rem(sp + 1, H)),
            device_id_type=MESH,
        )

    return_copy(orecv, 0).wait_recv()

    @pl.loop(0, BAGS // 2)
    def _(rp):
        halves = []
        for r in range(2):
            moved = []
            for h in range(H):
                block = orecv[(2 * rp + r) * H + h].astype(F32)
                tail = jnp.where(
                    lane32 < 128 - HD,
                    pltpu.roll(block[0:8], 128 - HD, 1),
                    pltpu.roll(block[8:16], 112, 1),
                )
                whole = jnp.concatenate([block, tail], axis=0)
                shift = HD * h % 128
                moved.append(pltpu.roll(whole, shift, 1) if shift else whole)
            columns = []
            for j in range(D // 128):
                first = 128 * j // HD
                column = moved[first]
                for h in range(first + 1, H):
                    if HD * h >= 128 * (j + 1):
                        break
                    column = jnp.where(lane < HD * h - 128 * j, column, moved[h])
                columns.append(column)
            halves.append(columns)
        rows = pl.ds(pl.multiple_of(rp * 2 * CAP, 2 * CAP), 2 * CAP)
        for j in range(D // 128):
            att[rows, 128 * j : 128 * j + 128] = jnp.concatenate(
                [halves[0][j], halves[1][j]], axis=0
            ).astype(BF16)

    copy_out.wait()
    wide[:, 0:D] = jnp.dot(att[...], wbig[:, 0:D], preferred_element_type=F32)

    @pl.loop(0, BAGS // 2)
    def _(r):
        rows = pl.ds(pl.multiple_of(r * 2 * CAP, 2 * CAP), 2 * CAP)
        hidden = (xs[rows, :] + two_mods(mod_ref, r, 2) * wide[rows, 0:D]).astype(BF16).astype(F32)
        xs[rows, :] = hidden
        norms[rows, :] = (
            norm(hidden) * (1.0 + two_mods(mod_ref, r, 4)) + two_mods(mod_ref, r, 3)
        ).astype(BF16)

    copy_fc1.wait()
    for part in range(2):
        inner = jnp.dot(
            norms[...], wbig[:, D * (part + 1) : D * (part + 2)], preferred_element_type=F32
        )
        act[:, D * part : D * (part + 1)] = jax.nn.gelu(inner, approximate=True).astype(BF16)
    copy_fc2.wait()
    wide[:, 0:D] = jnp.dot(act[...], wfc2[...], preferred_element_type=F32)

    @pl.loop(0, BAGS // 2)
    def _(r):
        rows = pl.ds(pl.multiple_of(r * 2 * CAP, 2 * CAP), 2 * CAP)
        att[rows, :] = (xs[rows, :] + two_mods(mod_ref, r, 5) * wide[rows, 0:D]).astype(BF16)

    out_ref[...] = lax.dot_general(
        place[...], att[...], (((0,), (0,)), ((), ())), preferred_element_type=F32
    ).astype(BF16)

    for g in range(GROUPS):
        group_copy(g).wait_send()
    return_copy(osend, 1).wait_send()


def fused(tokens, row_seq, modulation, w_qkv, w_out, w_fc1, w_fc2):
    vmem = pl.BlockSpec(memory_space=pltpu.VMEM)
    anywhere = pl.BlockSpec(memory_space=pl.ANY)
    return pl.pallas_call(
        kernel,
        out_shape=[
            jax.ShapeDtypeStruct((ROWS, D), BF16),
            jax.ShapeDtypeStruct((8, 128), F32),
        ],
        in_specs=[vmem, vmem, vmem, anywhere, anywhere, anywhere, anywhere],
        out_specs=[vmem, vmem],
        scratch_shapes=[
            pltpu.VMEM((D, 3 * D), BF16),
            pltpu.VMEM((FF, D), BF16),
            pltpu.VMEM((DEVS, 2 * CAP, 128), BF16),
            pltpu.VMEM((DEVS, 2 * CAP, 128), BF16),
            pltpu.VMEM((KEYS, 128), BF16),
            pltpu.VMEM((WIDE, KEYS), BF16),
            pltpu.VMEM((KEYS, 128), BF16),
            pltpu.VMEM((WIDE, KEYS), F32),
            pltpu.VMEM((GROWS, 128), F32),
            pltpu.VMEM((8, 128), F32),
            pltpu.VMEM((SLOTS, 3 * D), F32),
            pltpu.VMEM((SLOTS, D), F32),
            pltpu.VMEM((SLOTS, D), BF16),
            pltpu.VMEM((SLOTS, D), BF16),
            pltpu.VMEM((SLOTS, FF), BF16),
            pltpu.VMEM((SLOTS, ROWS), BF16),
            pltpu.VMEM((SLOTS, 128), F32),
            pltpu.VMEM((DEVS, 32, 128), BF16),
            pltpu.VMEM((DEVS, 32, 128), BF16),
            pltpu.SemaphoreType.DMA((4,)),
            pltpu.SemaphoreType.DMA((GROUPS,)),
            pltpu.SemaphoreType.DMA((GROUPS,)),
            pltpu.SemaphoreType.DMA,
            pltpu.SemaphoreType.DMA,
        ],
        compiler_params=pltpu.CompilerParams(
            collective_id=0, has_side_effects=True, vmem_limit_bytes=62 * 2**20
        ),
    )(tokens, row_seq.reshape(1, ROWS), jnp.swapaxes(modulation, 0, 1), w_qkv, w_out, w_fc1, w_fc2)


def layer_norm(values):
    center = values - jnp.mean(values, axis=-1, keepdims=True)
    spread = jnp.mean(center * center, axis=-1, keepdims=True)
    return center * lax.rsqrt(spread + EPS)


def lookup(seq_codes, modulation):
    seq_total = modulation.shape[0]
    one_hot = (seq_codes[:, None] == jnp.arange(seq_total, dtype=jnp.int32)[None, :]).astype(
        jnp.float32
    )
    table_rows = modulation.reshape(seq_total, -1)
    picked = jnp.dot(
        one_hot, table_rows, precision=lax.Precision.HIGHEST, preferred_element_type=jnp.float32
    )
    return picked.reshape(seq_codes.shape[0], 6, -1)


def project(source_rows, mods, w_qkv):
    normed = (layer_norm(source_rows.astype(jnp.float32)) * (1.0 + mods[:, 1]) + mods[:, 0]).astype(
        jnp.bfloat16
    )
    return jnp.dot(normed, w_qkv, preferred_element_type=jnp.float32).astype(jnp.bfloat16)


def attend(packed, seq_codes):
    key_count = packed.shape[0]
    local_width = packed.shape[2]
    head_local = local_width // HD
    queries = packed[:, 0].reshape(key_count, head_local, HD)
    key_rows = packed[:, 1].reshape(key_count, head_local, HD)
    values = packed[:, 2].reshape(key_count, head_local, HD)
    block_size = math.gcd(key_count, 512)
    score_scale = 1.0 / math.sqrt(HD)

    def one_block(block_index):
        first_row = block_index * block_size
        query_part = lax.dynamic_slice_in_dim(queries, first_row, block_size, 0)
        query_seq = lax.dynamic_slice_in_dim(seq_codes, first_row, block_size, 0)
        scores = (
            jnp.einsum("qhd,khd->hqk", query_part, key_rows, preferred_element_type=jnp.float32)
            * score_scale
        )
        allowed = query_seq[:, None] == seq_codes[None, :]
        scores = jnp.where(allowed[None], scores, -jnp.inf)
        row_max = jnp.max(scores, axis=-1, keepdims=True)
        raised = jnp.exp(scores - row_max)
        denominator = jnp.sum(raised, axis=-1)
        probs = raised.astype(jnp.bfloat16)
        mixed_rows = jnp.einsum("hqk,khd->qhd", probs, values, preferred_element_type=jnp.float32)
        mixed_rows = mixed_rows / jnp.transpose(denominator)[:, :, None]
        return mixed_rows.astype(jnp.bfloat16).reshape(block_size, local_width)

    blocks = lax.map(one_block, jnp.arange(key_count // block_size, dtype=jnp.int32))
    return blocks.reshape(key_count, local_width)


def finish(residual, attended, mods, w_out, w_fc1, w_fc2):
    branch = jnp.dot(attended, w_out, preferred_element_type=jnp.float32)
    hidden = (residual.astype(jnp.float32) + mods[:, 2] * branch).astype(jnp.bfloat16)
    normed = (layer_norm(hidden.astype(jnp.float32)) * (1.0 + mods[:, 4]) + mods[:, 3]).astype(
        jnp.bfloat16
    )
    active = jax.nn.gelu(
        jnp.dot(normed, w_fc1, preferred_element_type=jnp.float32), approximate=True
    ).astype(jnp.bfloat16)
    return (
        hidden.astype(jnp.float32)
        + mods[:, 5] * jnp.dot(active, w_fc2, preferred_element_type=jnp.float32)
    ).astype(jnp.bfloat16)


def plan_with_maximum(tokens, row_seq, modulation, w_qkv, w_out, w_fc1, w_fc2):
    bag_count = lax.axis_size("bag")
    sp_count = lax.axis_size("sp")
    row_count, model_width = tokens.shape
    capacity = row_count // bag_count * 5 // 4
    slot_count = bag_count * capacity
    local_width = model_width // sp_count
    key_count = sp_count * slot_count
    bag_of = row_seq
    member = (bag_of[:, None] == jnp.arange(bag_count, dtype=jnp.int32)[None, :]).astype(jnp.int32)
    before = jnp.cumsum(member, axis=0) - member
    rank_in = jnp.sum(before * member, axis=1)
    position = bag_of * capacity + rank_in
    source_row = (
        jnp.zeros((slot_count,), jnp.int32).at[position].set(jnp.arange(row_count, dtype=jnp.int32))
    )
    filled = jnp.zeros((slot_count,), jnp.bool_).at[position].set(True)
    slot_seq = jnp.where(filled, jnp.take(row_seq, source_row), -1)
    send_rows = jnp.where(
        filled[:, None], jnp.take(tokens, source_row, axis=0), jnp.zeros((), jnp.bfloat16)
    )
    arrived, arrived_seq = (
        lax.all_to_all(send_rows, "bag", split_axis=0, concat_axis=0, tiled=True),
        lax.all_to_all(
            slot_seq.astype(jnp.bfloat16), "bag", split_axis=0, concat_axis=0, tiled=True
        ),
    )
    mods = lookup(arrived_seq.astype(jnp.int32), modulation)
    packed = project(arrived, mods, w_qkv).reshape(slot_count, 3, sp_count, local_width)
    code_copies = jnp.broadcast_to(arrived_seq[:, None, None, None], (slot_count, 1, sp_count, 1))
    by_head, head_seq = (
        lax.all_to_all(packed, "sp", split_axis=2, concat_axis=0, tiled=True),
        lax.all_to_all(code_copies, "sp", split_axis=2, concat_axis=0, tiled=True),
    )
    attended = attend(
        by_head.reshape(key_count, 3, local_width), head_seq.reshape(key_count).astype(jnp.int32)
    )
    by_slot = lax.all_to_all(
        attended.reshape(key_count, 1, local_width), "sp", split_axis=0, concat_axis=1, tiled=True
    )
    finished = finish(arrived, by_slot.reshape(slot_count, model_width), mods, w_out, w_fc1, w_fc2)
    returned = lax.all_to_all(finished, "bag", split_axis=0, concat_axis=0, tiled=True)
    return jnp.take(returned, position, axis=0)


def shards(*operands):
    output, bound = fused(*operands)
    product = bound[0, QLANE] * bound[0, QLANE + 1]
    return lax.cond(
        product < LIMIT * LIMIT, lambda kept, *rest: kept, lambda _, *rest: plan_with_maximum(*rest), output, *operands
    )


def solution(mesh):
    placed = (P(("bag", "sp"), None), P(("bag", "sp")), P(), P(), P(), P(), P())
    return jax.shard_map(
        shards, mesh=mesh, in_specs=placed, out_specs=P(("bag", "sp"), None), check_vma=False
    )
```

```python
import functools
import math

import jax
import jax.numpy as jnp
from jax import lax
from jax.experimental import pallas as pl
from jax.experimental.pallas import tpu as pltpu
from jax.sharding import PartitionSpec as P

MESH = pl.DeviceIdType.MESH
D = 1152
H = 16
HD = 72
FF = 2304
BAGS = 8
CAP = 40
ROWS = 256
SLOTS = BAGS * CAP
DEVS = 128
GROUPS = 4
BOTH = (0, 1)
STAGES = (
    (0, BOTH, 0, 32), (1, BOTH, 32, 32), (2, BOTH, 64, 32), (3, BOTH, 96, 32),
)
PER = DEVS // GROUPS
GROWS = PER * CAP
KEYS = DEVS * CAP
WIDE = 80
LIMIT = 90.0
QHEAD = 55
QLANE = 96
EPS = 1e-6
BIG = 1e30
F32 = jnp.float32
BF16 = jnp.bfloat16


def peers(g, dy, sign):
    bag, sp = lax.axis_index("bag"), lax.axis_index("sp")
    x, c, z, y = bag // 2, lax.rem(bag, 2), sp // 4, lax.rem(sp, 4)
    row = lax.rem(y + 4 + sign * dy, 4)
    cores = [c, 1 - c]
    found = []
    for dx in range(4):
        bags = lax.rem(x + 4 + sign * dx, 4) * 2
        heads = lax.rem(z + 8 + sign * (g - dx - dy), 4) * 4 + row
        for dc in BOTH:
            found.append((dc, dc * 16 + dy * 4 + dx, (bags + cores[dc], heads)))
    return found


def each_row(g, sign, act, wanted):
    def one_row(dy, carry):
        act([(i, device) for dc, i, device in peers(g, dy, sign) if dc in wanted])
        return carry

    low = 0
    if g == 0:
        act([(i, device) for dc, i, device in peers(g, 0, sign) if dc in wanted and i])
        low = 1
    lax.fori_loop(low, 4, one_row, 0)


def norm(values):
    center = values - jnp.mean(values, axis=-1, keepdims=True)
    spread = jnp.mean(center * center, axis=-1, keepdims=True)
    return center * lax.rsqrt(spread + EPS)


def two_mods(mod_ref, r, which):
    return jnp.concatenate(
        [
            jnp.broadcast_to(mod_ref[which, pl.ds(2 * r, 1), :], (CAP, D)),
            jnp.broadcast_to(mod_ref[which, pl.ds(2 * r + 1, 1), :], (CAP, D)),
        ],
        axis=0,
    )


def kernel(
    tok_ref, seq_ref, mod_ref, wqkv_hbm, wout_hbm, wfc1_hbm, wfc2_hbm, out_ref, place, safe_ref,
    wbig, wfc2, send, recv, kbuf, vbuf, qbuf, acc_s, stage, peak, wide, xs, norms, att, act, bound_ref,
    bias_s, osend, orecv, w_sem, ssem, rsem, ssem2, rsem2,
):
    bag, sp = lax.axis_index("bag"), lax.axis_index("sp")
    me = bag * H + sp
    barrier = pltpu.get_barrier_semaphore()

    copy_qkv = pltpu.make_async_copy(wqkv_hbm, wbig, w_sem.at[0])
    copy_qkv.start()
    copy_fc2 = pltpu.make_async_copy(wfc2_hbm, wfc2, w_sem.at[1])
    copy_fc2.start()

    def greet(device):
        pl.semaphore_signal(barrier, inc=1, device_id=device, device_id_type=MESH)

    for g in range(1, GROUPS):
        greet(peers(g, 0, 1)[0][2])

    seq = seq_ref[...]
    member = (lax.broadcasted_iota(jnp.int32, (BAGS, ROWS), 0) == seq).astype(F32)
    earlier = (
        lax.broadcasted_iota(jnp.int32, (ROWS, ROWS), 0)
        < lax.broadcasted_iota(jnp.int32, (ROWS, ROWS), 1)
    ).astype(BF16)
    before = jnp.dot(member.astype(BF16), earlier, preferred_element_type=F32)
    rank = jnp.sum(member * before, axis=0, keepdims=True)
    position = seq.astype(F32) * CAP + rank
    one_hot = (
        lax.broadcasted_iota(jnp.int32, (SLOTS, ROWS), 0).astype(F32) == position
    ).astype(F32)
    bias_s[...] = jnp.broadcast_to(
        (jnp.sum(one_hot, axis=1, keepdims=True) - 1.0) * BIG, (SLOTS, 128)
    )
    place[...] = one_hot.astype(BF16)
    xs[...] = jnp.dot(place[...], tok_ref[...], preferred_element_type=F32)

    @pl.loop(0, BAGS // 2)
    def _(r):
        for dy in range(4):
            for _, i, device in peers(r, dy, 1):
                if i:
                    greet(device)
        rows = pl.ds(pl.multiple_of(r * 2 * CAP, 2 * CAP), 2 * CAP)
        norms[rows, :] = (
            norm(xs[rows, :]) * (1.0 + two_mods(mod_ref, r, 1)) + two_mods(mod_ref, r, 0)
        ).astype(BF16)

    copy_qkv.wait()
    scale = math.log2(math.e) / math.sqrt(HD)
    for part in range(3):
        cols = pl.ds(part * D, D)
        wide[:, cols] = jnp.dot(norms[...], wbig[:, cols], preferred_element_type=F32) * (
            scale if part == 0 else 1.0
        )
    feature = lax.broadcasted_iota(jnp.int32, (2 * D, 128), 0)
    first = lax.broadcasted_iota(jnp.int32, (2 * D, 128), 1) * HD
    segment = ((feature >= first) & (feature < first + HD)).astype(BF16)
    squares = wide[:, 0 : 2 * D]
    lengths = 1.02 * jnp.dot(
        (squares * squares).astype(BF16), segment, preferred_element_type=F32
    )
    longest = jnp.max(lengths, axis=0, keepdims=True)
    lane1 = lax.broadcasted_iota(jnp.int32, (1, 128), 1)
    long_q = jnp.max(jnp.where(lane1 < H, longest, 0.0), axis=1, keepdims=True)
    long_k = jnp.max(jnp.where(lane1 >= H, longest, 0.0), axis=1, keepdims=True)
    peak[0:1, :] = jnp.where(lane1 == QLANE, long_q, jnp.where(lane1 == QLANE + 1, long_k, 0.0))
    copy_out = pltpu.make_async_copy(wout_hbm, wbig.at[:, pl.ds(0, D)], w_sem.at[2])
    copy_out.start()
    copy_fc1 = pltpu.make_async_copy(wfc1_hbm, wbig.at[:, pl.ds(D, FF)], w_sem.at[3])
    copy_fc1.start()

    lane = lax.broadcasted_iota(jnp.int32, (CAP, 128), 1)

    @pl.loop(0, BAGS)
    def _(r):
        rows = pl.ds(pl.multiple_of(r * CAP, 8), CAP)

        def piece(column, width, target):
            first, off = column // 128 * 128, column % 128
            shift = (target - off) % 128
            main = wide[rows, first : first + 128]
            if shift:
                main = pltpu.roll(main, shift, 1)
            if off + width > 128:
                rest = wide[rows, first + 128 : first + 256]
                if shift:
                    rest = pltpu.roll(rest, shift, 1)
                main = jnp.where(lane < target + 128 - off, main, rest)
            return main

        bias = bias_s[rows, :]
        lengths = jnp.broadcast_to(peak[0:1, :], (CAP, 128))
        for h in range(H):
            keys = jnp.where(lane < HD, piece(D + HD * h, HD, 0), piece(HD * h, QHEAD, HD + 1))
            keys = jnp.where(lane == HD, bias, keys)
            values = jnp.where(
                lane < HD,
                piece(2 * D + HD * h, HD, 0),
                piece(HD * h + QHEAD, HD - QHEAD, HD + 1),
            )
            values = jnp.where(lane == HD, 1.0, values)
            values = jnp.where(lane < HD + 1 + HD - QHEAD, values, lengths)
            send[r * H + h] = jnp.concatenate([keys, values], axis=0).astype(BF16)

    pl.semaphore_wait(barrier, DEVS - 1)
    def push_stage(stage):
        g, cores, _, _ = STAGES[stage]

        def push(row):
            for i, device in row:
                pltpu.make_async_remote_copy(
                    src_ref=send.at[device[0] * H + device[1]],
                    dst_ref=recv.at[g * PER + i],
                    send_sem=ssem.at[stage],
                    recv_sem=rsem.at[stage],
                    device_id=device,
                    device_id_type=MESH,
                ).start()

        each_row(g, 1, push, cores)

    push_stage(0)
    push_stage(1)
    push_stage(2)
    recv[0] = send[me]

    def stage_copy(stage):
        _, _, first, count = STAGES[stage]
        skip = 1 if stage == 0 else 0
        block = recv.at[pl.ds(first + skip, count - skip)]
        return pltpu.make_async_remote_copy(
            src_ref=block,
            dst_ref=block,
            send_sem=ssem.at[stage],
            recv_sem=rsem.at[stage],
            device_id=(bag, lax.rem(sp + 1, H)),
            device_id_type=MESH,
        )

    lane2 = lax.broadcasted_iota(jnp.int32, (2 * CAP, 128), 1)

    def unpack(source, count):
        def two(n, top):
            one = recv[2 * n].astype(F32)
            two = recv[2 * n + 1].astype(F32)
            keys = jnp.concatenate([one[:CAP], two[:CAP]], axis=0)
            values = jnp.concatenate([one[CAP:], two[CAP:]], axis=0)
            query = jnp.where(
                lane2 < QHEAD,
                pltpu.roll(keys, 127 - HD, 1),
                pltpu.roll(values, (QHEAD - HD - 1) % 128, 1),
            )
            query = jnp.where(lane2 < HD, query, jnp.where(lane2 == HD, 1.0, 0.0))
            rows = pl.ds(pl.multiple_of(n * 2 * CAP, 2 * CAP), 2 * CAP)
            kbuf[rows, :] = keys.astype(BF16)
            qbuf[rows, :] = query.astype(BF16)
            near = pl.ds(pl.multiple_of((n - source // 2) * 2 * CAP, 2 * CAP), 2 * CAP)
            stage[near, :] = values
            return jnp.maximum(top, values)

        top = lax.fori_loop(
            source // 2, (source + count) // 2, two, jnp.zeros((2 * CAP, 128), F32), unroll=8
        )
        bound_ref[...] = jnp.maximum(
            bound_ref[...], jnp.broadcast_to(jnp.max(top, axis=0, keepdims=True), (8, 128))
        )
        vbuf[:, source * CAP : (source + count) * CAP] = (
            stage[0 : count * CAP, :].T[0:WIDE].astype(BF16)
        )

    def attend(first, rows, key_first, key_rows):
        keys = pl.ds(key_first, key_rows)
        queries = slice(first, first + rows)
        scores = lax.dot_general(
            kbuf[keys, :], qbuf[queries, :], (((1,), (1,)), ((), ())), preferred_element_type=F32
        )
        acc_s[:, queries] += jnp.dot(
            vbuf[:, keys], jnp.exp2(scores).astype(BF16), preferred_element_type=F32
        )

    lane32 = lax.broadcasted_iota(jnp.int32, (8, 128), 1)

    def give_back(stage_of):
        g, cores, source, count = STAGES[stage_of]
        mixed = acc_s[:, source * CAP : (source + count) * CAP]
        mixed = mixed * (1.0 / mixed[HD : HD + 1, :])
        stage[0 : count * CAP, :] = jnp.concatenate(
            [mixed, jnp.zeros((128 - WIDE, count * CAP), F32)], axis=0
        ).T

        def packed(i):
            near = pl.multiple_of((g * PER + i - source) * CAP, 8)
            mixed = stage[pl.ds(near, CAP), :]
            tail = mixed[32:40]
            return jnp.concatenate(
                [
                    jnp.where(lane32 < HD, mixed[0:8], pltpu.roll(tail, HD, 1)),
                    jnp.where(lane32 < HD, mixed[8:16], pltpu.roll(tail, 16, 1)),
                    mixed[16:32],
                ],
                axis=0,
            ).astype(BF16)

        def push(row):
            for i, _ in row:
                osend[g * PER + i] = packed(i)
            for i, device in row:
                pltpu.make_async_remote_copy(
                    src_ref=osend.at[g * PER + i],
                    dst_ref=orecv.at[me],
                    send_sem=ssem2,
                    recv_sem=rsem2,
                    device_id=device,
                    device_id_type=MESH,
                ).start()

        each_row(g, -1, push, cores)
        if stage_of == 0:
            orecv[me] = packed(0)

    acc_s[...] = jnp.zeros((WIDE, KEYS), F32)
    bound_ref[...] = jnp.zeros((8, 128), F32)
    for n, (_, _, source, count) in enumerate(STAGES):
        stage_copy(n).wait_recv()
        if n == 0:
            push_stage(3)
        unpack(source, count)
        last = n == len(STAGES) - 1
        for t in range(n):
            attend(STAGES[t][2] * CAP, STAGES[t][3] * CAP, source * CAP, count * CAP)
            if last:
                give_back(t)
        whole = (source + count) // PER

        @pl.loop(0, whole)
        def _(k, source=source, count=count):
            attend(source * CAP, count * CAP, pl.multiple_of(k * GROWS, GROWS), GROWS)

        if whole * PER < source + count:
            attend(source * CAP, count * CAP, source * CAP, count * CAP)
        if last:
            give_back(n)

    def return_copy(buf, lo):
        block = buf.at[pl.ds(lo, DEVS - 1)]
        return pltpu.make_async_remote_copy(
            src_ref=block,
            dst_ref=block,
            send_sem=ssem2,
            recv_sem=rsem2,
            device_id=(bag, lax.rem(sp + 1, H)),
            device_id_type=MESH,
        )

    return_copy(orecv, 0).wait_recv()

    @pl.loop(0, BAGS // 2)
    def _(rp):
        halves = []
        for r in range(2):
            moved = []
            for h in range(H):
                block = orecv[(2 * rp + r) * H + h].astype(F32)
                tail = jnp.where(
                    lane32 < 128 - HD,
                    pltpu.roll(block[0:8], 128 - HD, 1),
                    pltpu.roll(block[8:16], 112, 1),
                )
                whole = jnp.concatenate([block, tail], axis=0)
                shift = HD * h % 128
                moved.append(pltpu.roll(whole, shift, 1) if shift else whole)
            columns = []
            for j in range(D // 128):
                first = 128 * j // HD
                column = moved[first]
                for h in range(first + 1, H):
                    if HD * h >= 128 * (j + 1):
                        break
                    column = jnp.where(lane < HD * h - 128 * j, column, moved[h])
                columns.append(column)
            halves.append(columns)
        rows = pl.ds(pl.multiple_of(rp * 2 * CAP, 2 * CAP), 2 * CAP)
        for j in range(D // 128):
            att[rows, 128 * j : 128 * j + 128] = jnp.concatenate(
                [halves[0][j], halves[1][j]], axis=0
            ).astype(BF16)

    copy_out.wait()
    wide[:, 0:D] = jnp.dot(att[...], wbig[:, 0:D], preferred_element_type=F32)

    @pl.loop(0, BAGS // 2)
    def _(r):
        rows = pl.ds(pl.multiple_of(r * 2 * CAP, 2 * CAP), 2 * CAP)
        hidden = (xs[rows, :] + two_mods(mod_ref, r, 2) * wide[rows, 0:D]).astype(BF16).astype(F32)
        xs[rows, :] = hidden
        norms[rows, :] = (
            norm(hidden) * (1.0 + two_mods(mod_ref, r, 4)) + two_mods(mod_ref, r, 3)
        ).astype(BF16)

    copy_fc1.wait()
    copy_fc2.wait()
    width = FF // 3

    def inner(part):
        first = D + width * part
        return jnp.dot(
            norms[...], wbig[:, first : first + width], preferred_element_type=F32
        )

    now = inner(0)
    for part in range(3):
        later = inner(part + 1) if part < 2 else None
        act[:, width * part : width * (part + 1)] = jax.nn.gelu(now, approximate=True).astype(BF16)
        now = later
    wide[:, 0:D] = jnp.dot(act[...], wfc2[...], preferred_element_type=F32)

    @pl.loop(0, BAGS // 2)
    def _(r):
        rows = pl.ds(pl.multiple_of(r * 2 * CAP, 2 * CAP), 2 * CAP)
        out_ref[rows, :] = (xs[rows, :] + two_mods(mod_ref, r, 5) * wide[rows, 0:D]).astype(BF16)

    top = bound_ref[0:1, :]
    long_q = jnp.max(jnp.where(lane1 == QLANE, top, 0.0))
    long_k = jnp.max(jnp.where(lane1 == QLANE + 1, top, 0.0))
    safe_ref[0, 0] = (long_q * long_k < LIMIT * LIMIT).astype(jnp.int32)

    for n in range(len(STAGES)):
        stage_copy(n).wait_send()
    return_copy(osend, 1).wait_send()


def fused(tokens, row_seq, modulation, w_qkv, w_out, w_fc1, w_fc2):
    vmem = pl.BlockSpec(memory_space=pltpu.VMEM)
    anywhere = pl.BlockSpec(memory_space=pl.ANY)
    return pl.pallas_call(
        kernel,
        out_shape=[
            jax.ShapeDtypeStruct((SLOTS, D), BF16),
            jax.ShapeDtypeStruct((SLOTS, ROWS), BF16),
            jax.ShapeDtypeStruct((1, 1), jnp.int32),
        ],
        in_specs=[vmem, vmem, vmem, anywhere, anywhere, anywhere, anywhere],
        out_specs=[vmem, vmem, pl.BlockSpec(memory_space=pltpu.SMEM)],
        scratch_shapes=[
            pltpu.VMEM((D, 3 * D), BF16),
            pltpu.VMEM((FF, D), BF16),
            pltpu.VMEM((DEVS, 2 * CAP, 128), BF16),
            pltpu.VMEM((DEVS, 2 * CAP, 128), BF16),
            pltpu.VMEM((KEYS, 128), BF16),
            pltpu.VMEM((WIDE, KEYS), BF16),
            pltpu.VMEM((KEYS, 128), BF16),
            pltpu.VMEM((WIDE, KEYS), F32),
            pltpu.VMEM((GROWS, 128), F32),
            pltpu.VMEM((8, 128), F32),
            pltpu.VMEM((SLOTS, 3 * D), F32),
            pltpu.VMEM((SLOTS, D), F32),
            pltpu.VMEM((SLOTS, D), BF16),
            pltpu.VMEM((SLOTS, D), BF16),
            pltpu.VMEM((SLOTS, FF), BF16),
            pltpu.VMEM((8, 128), F32),
            pltpu.VMEM((SLOTS, 128), F32),
            pltpu.VMEM((DEVS, 32, 128), BF16),
            pltpu.VMEM((DEVS, 32, 128), BF16),
            pltpu.SemaphoreType.DMA((4,)),
            pltpu.SemaphoreType.DMA((len(STAGES),)),
            pltpu.SemaphoreType.DMA((len(STAGES),)),
            pltpu.SemaphoreType.DMA,
            pltpu.SemaphoreType.DMA,
        ],
        compiler_params=pltpu.CompilerParams(
            collective_id=0, has_side_effects=True, vmem_limit_bytes=62 * 2**20
        ),
    )(tokens, row_seq.reshape(1, ROWS), jnp.swapaxes(modulation, 0, 1), w_qkv, w_out, w_fc1, w_fc2)


def layer_norm(values):
    center = values - jnp.mean(values, axis=-1, keepdims=True)
    spread = jnp.mean(center * center, axis=-1, keepdims=True)
    return center * lax.rsqrt(spread + EPS)


def lookup(seq_codes, modulation):
    seq_total = modulation.shape[0]
    one_hot = (seq_codes[:, None] == jnp.arange(seq_total, dtype=jnp.int32)[None, :]).astype(
        jnp.float32
    )
    table_rows = modulation.reshape(seq_total, -1)
    picked = jnp.dot(
        one_hot, table_rows, precision=lax.Precision.HIGHEST, preferred_element_type=jnp.float32
    )
    return picked.reshape(seq_codes.shape[0], 6, -1)


def project(source_rows, mods, w_qkv):
    normed = (layer_norm(source_rows.astype(jnp.float32)) * (1.0 + mods[:, 1]) + mods[:, 0]).astype(
        jnp.bfloat16
    )
    return jnp.dot(normed, w_qkv, preferred_element_type=jnp.float32).astype(jnp.bfloat16)


def attend(packed, seq_codes):
    key_count = packed.shape[0]
    local_width = packed.shape[2]
    head_local = local_width // HD
    queries = packed[:, 0].reshape(key_count, head_local, HD)
    key_rows = packed[:, 1].reshape(key_count, head_local, HD)
    values = packed[:, 2].reshape(key_count, head_local, HD)
    block_size = math.gcd(key_count, 512)
    score_scale = 1.0 / math.sqrt(HD)

    def one_block(block_index):
        first_row = block_index * block_size
        query_part = lax.dynamic_slice_in_dim(queries, first_row, block_size, 0)
        query_seq = lax.dynamic_slice_in_dim(seq_codes, first_row, block_size, 0)
        scores = (
            jnp.einsum("qhd,khd->hqk", query_part, key_rows, preferred_element_type=jnp.float32)
            * score_scale
        )
        allowed = query_seq[:, None] == seq_codes[None, :]
        scores = jnp.where(allowed[None], scores, -jnp.inf)
        row_max = jnp.max(scores, axis=-1, keepdims=True)
        raised = jnp.exp(scores - row_max)
        denominator = jnp.sum(raised, axis=-1)
        probs = raised.astype(jnp.bfloat16)
        mixed_rows = jnp.einsum("hqk,khd->qhd", probs, values, preferred_element_type=jnp.float32)
        mixed_rows = mixed_rows / jnp.transpose(denominator)[:, :, None]
        return mixed_rows.astype(jnp.bfloat16).reshape(block_size, local_width)

    blocks = lax.map(one_block, jnp.arange(key_count // block_size, dtype=jnp.int32))
    return blocks.reshape(key_count, local_width)


def finish(residual, attended, mods, w_out, w_fc1, w_fc2):
    branch = jnp.dot(attended, w_out, preferred_element_type=jnp.float32)
    hidden = (residual.astype(jnp.float32) + mods[:, 2] * branch).astype(jnp.bfloat16)
    normed = (layer_norm(hidden.astype(jnp.float32)) * (1.0 + mods[:, 4]) + mods[:, 3]).astype(
        jnp.bfloat16
    )
    active = jax.nn.gelu(
        jnp.dot(normed, w_fc1, preferred_element_type=jnp.float32), approximate=True
    ).astype(jnp.bfloat16)
    return (
        hidden.astype(jnp.float32)
        + mods[:, 5] * jnp.dot(active, w_fc2, preferred_element_type=jnp.float32)
    ).astype(jnp.bfloat16)


def plan_with_maximum(tokens, row_seq, modulation, w_qkv, w_out, w_fc1, w_fc2):
    bag_count = lax.axis_size("bag")
    sp_count = lax.axis_size("sp")
    row_count, model_width = tokens.shape
    capacity = row_count // bag_count * 5 // 4
    slot_count = bag_count * capacity
    local_width = model_width // sp_count
    key_count = sp_count * slot_count
    bag_of = row_seq
    member = (bag_of[:, None] == jnp.arange(bag_count, dtype=jnp.int32)[None, :]).astype(jnp.int32)
    before = jnp.cumsum(member, axis=0) - member
    rank_in = jnp.sum(before * member, axis=1)
    position = bag_of * capacity + rank_in
    source_row = (
        jnp.zeros((slot_count,), jnp.int32).at[position].set(jnp.arange(row_count, dtype=jnp.int32))
    )
    filled = jnp.zeros((slot_count,), jnp.bool_).at[position].set(True)
    slot_seq = jnp.where(filled, jnp.take(row_seq, source_row), -1)
    send_rows = jnp.where(
        filled[:, None], jnp.take(tokens, source_row, axis=0), jnp.zeros((), jnp.bfloat16)
    )
    arrived, arrived_seq = (
        lax.all_to_all(send_rows, "bag", split_axis=0, concat_axis=0, tiled=True),
        lax.all_to_all(
            slot_seq.astype(jnp.bfloat16), "bag", split_axis=0, concat_axis=0, tiled=True
        ),
    )
    mods = lookup(arrived_seq.astype(jnp.int32), modulation)
    packed = project(arrived, mods, w_qkv).reshape(slot_count, 3, sp_count, local_width)
    code_copies = jnp.broadcast_to(arrived_seq[:, None, None, None], (slot_count, 1, sp_count, 1))
    by_head, head_seq = (
        lax.all_to_all(packed, "sp", split_axis=2, concat_axis=0, tiled=True),
        lax.all_to_all(code_copies, "sp", split_axis=2, concat_axis=0, tiled=True),
    )
    attended = attend(
        by_head.reshape(key_count, 3, local_width), head_seq.reshape(key_count).astype(jnp.int32)
    )
    by_slot = lax.all_to_all(
        attended.reshape(key_count, 1, local_width), "sp", split_axis=0, concat_axis=1, tiled=True
    )
    finished = finish(arrived, by_slot.reshape(slot_count, model_width), mods, w_out, w_fc1, w_fc2)
    returned = lax.all_to_all(finished, "bag", split_axis=0, concat_axis=0, tiled=True)
    return jnp.take(returned, position, axis=0)


def in_row_order(slots, place, *_):
    return lax.dot_general(
        place, slots, (((0,), (0,)), ((), ())), preferred_element_type=jnp.float32
    ).astype(jnp.bfloat16)


def shards(*operands):
    slots, place, safe = fused(*operands)
    return lax.cond(
        safe[0, 0] == 1,
        in_row_order,
        lambda slots, place, *rest: plan_with_maximum(*rest),
        slots,
        place,
        *operands,
    )


def solution(mesh):
    placed = (P(("bag", "sp"), None), P(("bag", "sp")), P(), P(), P(), P(), P())
    return jax.shard_map(
        shards, mesh=mesh, in_specs=placed, out_specs=P(("bag", "sp"), None), check_vma=False
    )
```

```python
import functools
import math

import jax
import jax.numpy as jnp
from jax import lax
from jax.experimental import pallas as pl
from jax.experimental.pallas import tpu as pltpu
from jax.sharding import PartitionSpec as P

MESH = pl.DeviceIdType.MESH
D = 1152
H = 16
HD = 72
FF = 2304
BAGS = 8
CAP = 40
ROWS = 256
SLOTS = BAGS * CAP
DEVS = 128
GROUPS = 4
BOTH = (0, 1)
STAGES = (
    (0, BOTH, 0, 32), (1, BOTH, 32, 32), (2, BOTH, 64, 32), (3, BOTH, 96, 32),
)
PER = DEVS // GROUPS
GROWS = PER * CAP
KEYS = DEVS * CAP
WIDE = 80
LIMIT = 90.0
QHEAD = 55
QLANE = 96
EPS = 1e-6
BIG = 1e30
F32 = jnp.float32
BF16 = jnp.bfloat16


def peers(g, dy, sign):
    bag, sp = lax.axis_index("bag"), lax.axis_index("sp")
    x, c, z, y = bag // 2, lax.rem(bag, 2), sp // 4, lax.rem(sp, 4)
    row = lax.rem(y + 4 + sign * dy, 4)
    cores = [c, 1 - c]
    found = []
    for dx in range(4):
        bags = lax.rem(x + 4 + sign * dx, 4) * 2
        heads = lax.rem(z + 8 + sign * (g - dx - dy), 4) * 4 + row
        for dc in BOTH:
            found.append((dc, dc * 16 + dy * 4 + dx, (bags + cores[dc], heads)))
    return found


def each_row(g, sign, act, wanted):
    def one_row(dy, carry):
        act([(i, device) for dc, i, device in peers(g, dy, sign) if dc in wanted])
        return carry

    low = 0
    if g == 0:
        act([(i, device) for dc, i, device in peers(g, 0, sign) if dc in wanted and i])
        low = 1
    lax.fori_loop(low, 4, one_row, 0)


def norm(values):
    center = values - jnp.mean(values, axis=-1, keepdims=True)
    spread = jnp.mean(center * center, axis=-1, keepdims=True)
    return center * lax.rsqrt(spread + EPS)


def gelu(values):
    scale = -2.0 * math.sqrt(2.0 / math.pi) * math.log2(math.e)
    bent = values * (scale + (scale * 0.044715) * (values * values))
    return values / (1.0 + jnp.exp2(bent))


def two_mods(mod_ref, r, which):
    return jnp.concatenate(
        [
            jnp.broadcast_to(mod_ref[which, pl.ds(2 * r, 1), :], (CAP, D)),
            jnp.broadcast_to(mod_ref[which, pl.ds(2 * r + 1, 1), :], (CAP, D)),
        ],
        axis=0,
    )


def kernel(
    tok_ref, seq_ref, mod_ref, wqkv_hbm, wout_hbm, wfc1_hbm, wfc2_hbm, out_ref, place, safe_ref,
    wbig, wfc2, send, recv, kbuf, vbuf, qbuf, acc_s, stage, peak, wide, xs, norms, att, act, bound_ref,
    bias_s, osend, orecv, w_sem, ssem, rsem, ssem2, rsem2,
):
    bag, sp = lax.axis_index("bag"), lax.axis_index("sp")
    me = bag * H + sp
    barrier = pltpu.get_barrier_semaphore()

    copy_qkv = pltpu.make_async_copy(wqkv_hbm, wbig, w_sem.at[0])
    copy_qkv.start()
    copy_fc2 = pltpu.make_async_copy(wfc2_hbm, wfc2, w_sem.at[1])
    copy_fc2.start()

    def greet(device):
        pl.semaphore_signal(barrier, inc=1, device_id=device, device_id_type=MESH)

    for g in range(1, GROUPS):
        greet(peers(g, 0, 1)[0][2])

    seq = seq_ref[...]
    member = (lax.broadcasted_iota(jnp.int32, (BAGS, ROWS), 0) == seq).astype(F32)
    earlier = (
        lax.broadcasted_iota(jnp.int32, (ROWS, ROWS), 0)
        < lax.broadcasted_iota(jnp.int32, (ROWS, ROWS), 1)
    ).astype(BF16)
    before = jnp.dot(member.astype(BF16), earlier, preferred_element_type=F32)
    rank = jnp.sum(member * before, axis=0, keepdims=True)
    position = seq.astype(F32) * CAP + rank
    one_hot = (
        lax.broadcasted_iota(jnp.int32, (SLOTS, ROWS), 0).astype(F32) == position
    ).astype(F32)
    bias_s[...] = jnp.broadcast_to(
        (jnp.sum(one_hot, axis=1, keepdims=True) - 1.0) * BIG, (SLOTS, 128)
    )
    place[...] = one_hot.astype(BF16)
    xs[...] = jnp.dot(place[...], tok_ref[...], preferred_element_type=F32)

    @pl.loop(0, BAGS // 2)
    def _(r):
        for dy in range(4):
            for _, i, device in peers(r, dy, 1):
                if i:
                    greet(device)
        rows = pl.ds(pl.multiple_of(r * 2 * CAP, 2 * CAP), 2 * CAP)
        norms[rows, :] = (
            norm(xs[rows, :]) * (1.0 + two_mods(mod_ref, r, 1)) + two_mods(mod_ref, r, 0)
        ).astype(BF16)

    copy_qkv.wait()
    scale = math.log2(math.e) / math.sqrt(HD)
    for part in range(3):
        cols = pl.ds(part * D, D)
        wide[:, cols] = jnp.dot(norms[...], wbig[:, cols], preferred_element_type=F32) * (
            scale if part == 0 else 1.0
        )
    feature = lax.broadcasted_iota(jnp.int32, (2 * D, 128), 0)
    first = lax.broadcasted_iota(jnp.int32, (2 * D, 128), 1) * HD
    segment = ((feature >= first) & (feature < first + HD)).astype(BF16)
    squares = wide[:, 0 : 2 * D]
    lengths = 1.02 * jnp.dot(
        (squares * squares).astype(BF16), segment, preferred_element_type=F32
    )
    longest = jnp.max(lengths, axis=0, keepdims=True)
    lane1 = lax.broadcasted_iota(jnp.int32, (1, 128), 1)
    long_q = jnp.max(jnp.where(lane1 < H, longest, 0.0), axis=1, keepdims=True)
    long_k = jnp.max(jnp.where(lane1 >= H, longest, 0.0), axis=1, keepdims=True)
    peak[0:1, :] = jnp.where(lane1 == QLANE, long_q, jnp.where(lane1 == QLANE + 1, long_k, 0.0))
    copy_out = pltpu.make_async_copy(wout_hbm, wbig.at[:, pl.ds(0, D)], w_sem.at[2])
    copy_out.start()
    copy_fc1 = pltpu.make_async_copy(wfc1_hbm, wbig.at[:, pl.ds(D, FF)], w_sem.at[3])
    copy_fc1.start()

    lane = lax.broadcasted_iota(jnp.int32, (CAP, 128), 1)

    @pl.loop(0, BAGS)
    def _(r):
        rows = pl.ds(pl.multiple_of(r * CAP, 8), CAP)

        def piece(column, width, target):
            first, off = column // 128 * 128, column % 128
            shift = (target - off) % 128
            main = wide[rows, first : first + 128]
            if shift:
                main = pltpu.roll(main, shift, 1)
            if off + width > 128:
                rest = wide[rows, first + 128 : first + 256]
                if shift:
                    rest = pltpu.roll(rest, shift, 1)
                main = jnp.where(lane < target + 128 - off, main, rest)
            return main

        bias = bias_s[rows, :]
        lengths = jnp.broadcast_to(peak[0:1, :], (CAP, 128))
        for h in range(H):
            keys = jnp.where(lane < HD, piece(D + HD * h, HD, 0), piece(HD * h, QHEAD, HD + 1))
            keys = jnp.where(lane == HD, bias, keys)
            values = jnp.where(
                lane < HD,
                piece(2 * D + HD * h, HD, 0),
                piece(HD * h + QHEAD, HD - QHEAD, HD + 1),
            )
            values = jnp.where(lane == HD, 1.0, values)
            values = jnp.where(lane < HD + 1 + HD - QHEAD, values, lengths)
            send[r * H + h] = jnp.concatenate([keys, values], axis=0).astype(BF16)

    pl.semaphore_wait(barrier, DEVS - 1)
    def push_stage(stage):
        g, cores, _, _ = STAGES[stage]

        def push(row):
            for i, device in row:
                pltpu.make_async_remote_copy(
                    src_ref=send.at[device[0] * H + device[1]],
                    dst_ref=recv.at[g * PER + i],
                    send_sem=ssem.at[stage],
                    recv_sem=rsem.at[stage],
                    device_id=device,
                    device_id_type=MESH,
                ).start()

        each_row(g, 1, push, cores)

    push_stage(0)
    push_stage(1)
    push_stage(2)
    recv[0] = send[me]

    def stage_copy(stage):
        _, _, first, count = STAGES[stage]
        skip = 1 if stage == 0 else 0
        block = recv.at[pl.ds(first + skip, count - skip)]
        return pltpu.make_async_remote_copy(
            src_ref=block,
            dst_ref=block,
            send_sem=ssem.at[stage],
            recv_sem=rsem.at[stage],
            device_id=(bag, lax.rem(sp + 1, H)),
            device_id_type=MESH,
        )

    lane2 = lax.broadcasted_iota(jnp.int32, (2 * CAP, 128), 1)

    def unpack(source, count):
        def two(n, top):
            one = recv[2 * n].astype(F32)
            two = recv[2 * n + 1].astype(F32)
            keys = jnp.concatenate([one[:CAP], two[:CAP]], axis=0)
            values = jnp.concatenate([one[CAP:], two[CAP:]], axis=0)
            query = jnp.where(
                lane2 < QHEAD,
                pltpu.roll(keys, 127 - HD, 1),
                pltpu.roll(values, (QHEAD - HD - 1) % 128, 1),
            )
            query = jnp.where(lane2 < HD, query, jnp.where(lane2 == HD, 1.0, 0.0))
            rows = pl.ds(pl.multiple_of(n * 2 * CAP, 2 * CAP), 2 * CAP)
            kbuf[rows, :] = keys.astype(BF16)
            qbuf[rows, :] = query.astype(BF16)
            near = pl.ds(pl.multiple_of((n - source // 2) * 2 * CAP, 2 * CAP), 2 * CAP)
            stage[near, :] = values
            return jnp.maximum(top, values)

        top = lax.fori_loop(
            source // 2, (source + count) // 2, two, jnp.zeros((2 * CAP, 128), F32), unroll=8
        )
        bound_ref[...] = jnp.maximum(
            bound_ref[...], jnp.broadcast_to(jnp.max(top, axis=0, keepdims=True), (8, 128))
        )
        vbuf[:, source * CAP : (source + count) * CAP] = (
            stage[0 : count * CAP, :].T[0:WIDE].astype(BF16)
        )

    def attend(first, rows, key_first, key_rows):
        keys = pl.ds(key_first, key_rows)
        queries = slice(first, first + rows)
        scores = lax.dot_general(
            kbuf[keys, :], qbuf[queries, :], (((1,), (1,)), ((), ())), preferred_element_type=F32
        )
        acc_s[:, queries] += jnp.dot(
            vbuf[:, keys], jnp.exp2(scores).astype(BF16), preferred_element_type=F32
        )

    lane32 = lax.broadcasted_iota(jnp.int32, (8, 128), 1)

    def give_back(stage_of):
        g, cores, source, count = STAGES[stage_of]
        mixed = acc_s[:, source * CAP : (source + count) * CAP]
        mixed = mixed * (1.0 / mixed[HD : HD + 1, :])
        stage[0 : count * CAP, :] = jnp.concatenate(
            [mixed, jnp.zeros((128 - WIDE, count * CAP), F32)], axis=0
        ).T

        def packed(i):
            near = pl.multiple_of((g * PER + i - source) * CAP, 8)
            mixed = stage[pl.ds(near, CAP), :]
            tail = mixed[32:40]
            return jnp.concatenate(
                [
                    jnp.where(lane32 < HD, mixed[0:8], pltpu.roll(tail, HD, 1)),
                    jnp.where(lane32 < HD, mixed[8:16], pltpu.roll(tail, 16, 1)),
                    mixed[16:32],
                ],
                axis=0,
            ).astype(BF16)

        def push(row):
            for i, _ in row:
                osend[g * PER + i] = packed(i)
            for i, device in row:
                pltpu.make_async_remote_copy(
                    src_ref=osend.at[g * PER + i],
                    dst_ref=orecv.at[me],
                    send_sem=ssem2,
                    recv_sem=rsem2,
                    device_id=device,
                    device_id_type=MESH,
                ).start()

        each_row(g, -1, push, cores)
        if stage_of == 0:
            orecv[me] = packed(0)

    acc_s[...] = jnp.zeros((WIDE, KEYS), F32)
    bound_ref[...] = jnp.zeros((8, 128), F32)
    for n, (_, _, source, count) in enumerate(STAGES):
        stage_copy(n).wait_recv()
        if n == 0:
            push_stage(3)
        unpack(source, count)
        last = n == len(STAGES) - 1
        for t in range(n):
            attend(STAGES[t][2] * CAP, STAGES[t][3] * CAP, source * CAP, count * CAP)
            if last:
                give_back(t)
        whole = (source + count) // PER

        @pl.loop(0, whole)
        def _(k, source=source, count=count):
            attend(source * CAP, count * CAP, pl.multiple_of(k * GROWS, GROWS), GROWS)

        if whole * PER < source + count:
            attend(source * CAP, count * CAP, source * CAP, count * CAP)
        if last:
            give_back(n)

    def return_copy(buf, lo):
        block = buf.at[pl.ds(lo, DEVS - 1)]
        return pltpu.make_async_remote_copy(
            src_ref=block,
            dst_ref=block,
            send_sem=ssem2,
            recv_sem=rsem2,
            device_id=(bag, lax.rem(sp + 1, H)),
            device_id_type=MESH,
        )

    return_copy(orecv, 0).wait_recv()

    @pl.loop(0, BAGS // 2)
    def _(rp):
        halves = []
        for r in range(2):
            moved = []
            for h in range(H):
                block = orecv[(2 * rp + r) * H + h].astype(F32)
                tail = jnp.where(
                    lane32 < 128 - HD,
                    pltpu.roll(block[0:8], 128 - HD, 1),
                    pltpu.roll(block[8:16], 112, 1),
                )
                whole = jnp.concatenate([block, tail], axis=0)
                shift = HD * h % 128
                moved.append(pltpu.roll(whole, shift, 1) if shift else whole)
            columns = []
            for j in range(D // 128):
                first = 128 * j // HD
                column = moved[first]
                for h in range(first + 1, H):
                    if HD * h >= 128 * (j + 1):
                        break
                    column = jnp.where(lane < HD * h - 128 * j, column, moved[h])
                columns.append(column)
            halves.append(columns)
        rows = pl.ds(pl.multiple_of(rp * 2 * CAP, 2 * CAP), 2 * CAP)
        for j in range(D // 128):
            att[rows, 128 * j : 128 * j + 128] = jnp.concatenate(
                [halves[0][j], halves[1][j]], axis=0
            ).astype(BF16)

    copy_out.wait()
    wide[:, 0:D] = jnp.dot(att[...], wbig[:, 0:D], preferred_element_type=F32)

    @pl.loop(0, BAGS // 2, unroll=True)
    def _(r):
        rows = pl.ds(pl.multiple_of(r * 2 * CAP, 2 * CAP), 2 * CAP)
        hidden = (xs[rows, :] + two_mods(mod_ref, r, 2) * wide[rows, 0:D]).astype(BF16).astype(F32)
        xs[rows, :] = hidden
        norms[rows, :] = (
            norm(hidden) * (1.0 + two_mods(mod_ref, r, 4)) + two_mods(mod_ref, r, 3)
        ).astype(BF16)

    copy_fc1.wait()
    copy_fc2.wait()
    width = FF // 3

    def inner(part):
        first = D + width * part
        return jnp.dot(
            norms[...], wbig[:, first : first + width], preferred_element_type=F32
        )

    now = inner(0)
    for part in range(3):
        later = inner(part + 1) if part < 2 else None
        act[:, width * part : width * (part + 1)] = gelu(now).astype(BF16)
        now = later
    wide[:, 0:D] = jnp.dot(act[...], wfc2[...], preferred_element_type=F32)

    @pl.loop(0, BAGS // 2, unroll=True)
    def _(r):
        rows = pl.ds(pl.multiple_of(r * 2 * CAP, 2 * CAP), 2 * CAP)
        out_ref[rows, :] = (xs[rows, :] + two_mods(mod_ref, r, 5) * wide[rows, 0:D]).astype(BF16)

    top = bound_ref[0:1, :]
    long_q = jnp.max(jnp.where(lane1 == QLANE, top, 0.0))
    long_k = jnp.max(jnp.where(lane1 == QLANE + 1, top, 0.0))
    safe_ref[0, 0] = (long_q * long_k < LIMIT * LIMIT).astype(jnp.int32)

    for n in range(len(STAGES)):
        stage_copy(n).wait_send()
    return_copy(osend, 1).wait_send()


def fused(tokens, row_seq, modulation, w_qkv, w_out, w_fc1, w_fc2):
    vmem = pl.BlockSpec(memory_space=pltpu.VMEM)
    anywhere = pl.BlockSpec(memory_space=pl.ANY)
    return pl.pallas_call(
        kernel,
        out_shape=[
            jax.ShapeDtypeStruct((SLOTS, D), BF16),
            jax.ShapeDtypeStruct((SLOTS, ROWS), BF16),
            jax.ShapeDtypeStruct((1, 1), jnp.int32),
        ],
        in_specs=[vmem, vmem, vmem, anywhere, anywhere, anywhere, anywhere],
        out_specs=[vmem, vmem, pl.BlockSpec(memory_space=pltpu.SMEM)],
        scratch_shapes=[
            pltpu.VMEM((D, 3 * D), BF16),
            pltpu.VMEM((FF, D), BF16),
            pltpu.VMEM((DEVS, 2 * CAP, 128), BF16),
            pltpu.VMEM((DEVS, 2 * CAP, 128), BF16),
            pltpu.VMEM((KEYS, 128), BF16),
            pltpu.VMEM((WIDE, KEYS), BF16),
            pltpu.VMEM((KEYS, 128), BF16),
            pltpu.VMEM((WIDE, KEYS), F32),
            pltpu.VMEM((GROWS, 128), F32),
            pltpu.VMEM((8, 128), F32),
            pltpu.VMEM((SLOTS, 3 * D), F32),
            pltpu.VMEM((SLOTS, D), F32),
            pltpu.VMEM((SLOTS, D), BF16),
            pltpu.VMEM((SLOTS, D), BF16),
            pltpu.VMEM((SLOTS, FF), BF16),
            pltpu.VMEM((8, 128), F32),
            pltpu.VMEM((SLOTS, 128), F32),
            pltpu.VMEM((DEVS, 32, 128), BF16),
            pltpu.VMEM((DEVS, 32, 128), BF16),
            pltpu.SemaphoreType.DMA((4,)),
            pltpu.SemaphoreType.DMA((len(STAGES),)),
            pltpu.SemaphoreType.DMA((len(STAGES),)),
            pltpu.SemaphoreType.DMA,
            pltpu.SemaphoreType.DMA,
        ],
        compiler_params=pltpu.CompilerParams(
            collective_id=0, has_side_effects=True, vmem_limit_bytes=62 * 2**20
        ),
    )(tokens, row_seq.reshape(1, ROWS), jnp.swapaxes(modulation, 0, 1), w_qkv, w_out, w_fc1, w_fc2)


def layer_norm(values):
    center = values - jnp.mean(values, axis=-1, keepdims=True)
    spread = jnp.mean(center * center, axis=-1, keepdims=True)
    return center * lax.rsqrt(spread + EPS)


def lookup(seq_codes, modulation):
    seq_total = modulation.shape[0]
    one_hot = (seq_codes[:, None] == jnp.arange(seq_total, dtype=jnp.int32)[None, :]).astype(
        jnp.float32
    )
    table_rows = modulation.reshape(seq_total, -1)
    picked = jnp.dot(
        one_hot, table_rows, precision=lax.Precision.HIGHEST, preferred_element_type=jnp.float32
    )
    return picked.reshape(seq_codes.shape[0], 6, -1)


def project(source_rows, mods, w_qkv):
    normed = (layer_norm(source_rows.astype(jnp.float32)) * (1.0 + mods[:, 1]) + mods[:, 0]).astype(
        jnp.bfloat16
    )
    return jnp.dot(normed, w_qkv, preferred_element_type=jnp.float32).astype(jnp.bfloat16)


def attend(packed, seq_codes):
    key_count = packed.shape[0]
    local_width = packed.shape[2]
    head_local = local_width // HD
    queries = packed[:, 0].reshape(key_count, head_local, HD)
    key_rows = packed[:, 1].reshape(key_count, head_local, HD)
    values = packed[:, 2].reshape(key_count, head_local, HD)
    block_size = math.gcd(key_count, 512)
    score_scale = 1.0 / math.sqrt(HD)

    def one_block(block_index):
        first_row = block_index * block_size
        query_part = lax.dynamic_slice_in_dim(queries, first_row, block_size, 0)
        query_seq = lax.dynamic_slice_in_dim(seq_codes, first_row, block_size, 0)
        scores = (
            jnp.einsum("qhd,khd->hqk", query_part, key_rows, preferred_element_type=jnp.float32)
            * score_scale
        )
        allowed = query_seq[:, None] == seq_codes[None, :]
        scores = jnp.where(allowed[None], scores, -jnp.inf)
        row_max = jnp.max(scores, axis=-1, keepdims=True)
        raised = jnp.exp(scores - row_max)
        denominator = jnp.sum(raised, axis=-1)
        probs = raised.astype(jnp.bfloat16)
        mixed_rows = jnp.einsum("hqk,khd->qhd", probs, values, preferred_element_type=jnp.float32)
        mixed_rows = mixed_rows / jnp.transpose(denominator)[:, :, None]
        return mixed_rows.astype(jnp.bfloat16).reshape(block_size, local_width)

    blocks = lax.map(one_block, jnp.arange(key_count // block_size, dtype=jnp.int32))
    return blocks.reshape(key_count, local_width)


def finish(residual, attended, mods, w_out, w_fc1, w_fc2):
    branch = jnp.dot(attended, w_out, preferred_element_type=jnp.float32)
    hidden = (residual.astype(jnp.float32) + mods[:, 2] * branch).astype(jnp.bfloat16)
    normed = (layer_norm(hidden.astype(jnp.float32)) * (1.0 + mods[:, 4]) + mods[:, 3]).astype(
        jnp.bfloat16
    )
    active = jax.nn.gelu(
        jnp.dot(normed, w_fc1, preferred_element_type=jnp.float32), approximate=True
    ).astype(jnp.bfloat16)
    return (
        hidden.astype(jnp.float32)
        + mods[:, 5] * jnp.dot(active, w_fc2, preferred_element_type=jnp.float32)
    ).astype(jnp.bfloat16)


def plan_with_maximum(tokens, row_seq, modulation, w_qkv, w_out, w_fc1, w_fc2):
    bag_count = lax.axis_size("bag")
    sp_count = lax.axis_size("sp")
    row_count, model_width = tokens.shape
    capacity = row_count // bag_count * 5 // 4
    slot_count = bag_count * capacity
    local_width = model_width // sp_count
    key_count = sp_count * slot_count
    bag_of = row_seq
    member = (bag_of[:, None] == jnp.arange(bag_count, dtype=jnp.int32)[None, :]).astype(jnp.int32)
    before = jnp.cumsum(member, axis=0) - member
    rank_in = jnp.sum(before * member, axis=1)
    position = bag_of * capacity + rank_in
    source_row = (
        jnp.zeros((slot_count,), jnp.int32).at[position].set(jnp.arange(row_count, dtype=jnp.int32))
    )
    filled = jnp.zeros((slot_count,), jnp.bool_).at[position].set(True)
    slot_seq = jnp.where(filled, jnp.take(row_seq, source_row), -1)
    send_rows = jnp.where(
        filled[:, None], jnp.take(tokens, source_row, axis=0), jnp.zeros((), jnp.bfloat16)
    )
    arrived, arrived_seq = (
        lax.all_to_all(send_rows, "bag", split_axis=0, concat_axis=0, tiled=True),
        lax.all_to_all(
            slot_seq.astype(jnp.bfloat16), "bag", split_axis=0, concat_axis=0, tiled=True
        ),
    )
    mods = lookup(arrived_seq.astype(jnp.int32), modulation)
    packed = project(arrived, mods, w_qkv).reshape(slot_count, 3, sp_count, local_width)
    code_copies = jnp.broadcast_to(arrived_seq[:, None, None, None], (slot_count, 1, sp_count, 1))
    by_head, head_seq = (
        lax.all_to_all(packed, "sp", split_axis=2, concat_axis=0, tiled=True),
        lax.all_to_all(code_copies, "sp", split_axis=2, concat_axis=0, tiled=True),
    )
    attended = attend(
        by_head.reshape(key_count, 3, local_width), head_seq.reshape(key_count).astype(jnp.int32)
    )
    by_slot = lax.all_to_all(
        attended.reshape(key_count, 1, local_width), "sp", split_axis=0, concat_axis=1, tiled=True
    )
    finished = finish(arrived, by_slot.reshape(slot_count, model_width), mods, w_out, w_fc1, w_fc2)
    returned = lax.all_to_all(finished, "bag", split_axis=0, concat_axis=0, tiled=True)
    return jnp.take(returned, position, axis=0)


def in_row_order(slots, place, *_):
    return lax.dot_general(
        place, slots, (((0,), (0,)), ((), ())), preferred_element_type=jnp.float32
    ).astype(jnp.bfloat16)


def shards(*operands):
    slots, place, safe = fused(*operands)
    return lax.cond(
        safe[0, 0] == 1,
        in_row_order,
        lambda slots, place, *rest: plan_with_maximum(*rest),
        slots,
        place,
        *operands,
    )


def solution(mesh):
    placed = (P(("bag", "sp"), None), P(("bag", "sp")), P(), P(), P(), P(), P())
    return jax.shard_map(
        shards, mesh=mesh, in_specs=placed, out_specs=P(("bag", "sp"), None), check_vma=False
    )
```

```python
import functools
import math

import jax
import jax.numpy as jnp
from jax import lax
from jax.experimental import pallas as pl
from jax.experimental.pallas import tpu as pltpu
from jax.sharding import PartitionSpec as P

MESH = pl.DeviceIdType.MESH
D = 1152
H = 16
HD = 72
FF = 2304
BAGS = 8
CAP = 40
ROWS = 256
SLOTS = BAGS * CAP
DEVS = 128
GROUPS = 4
BOTH = (0, 1)
STAGES = (
    (0, BOTH, 0, 32), (1, BOTH, 32, 32), (2, BOTH, 64, 32), (3, BOTH, 96, 32),
)
PER = DEVS // GROUPS
GROWS = PER * CAP
KEYS = DEVS * CAP
WIDE = 80
LIMIT = 90.0
QHEAD = 55
QLANE = 96
EPS = 1e-6
BIG = 1e30
F32 = jnp.float32
BF16 = jnp.bfloat16


def peers(g, dy, sign):
    bag, sp = lax.axis_index("bag"), lax.axis_index("sp")
    x, c, z, y = bag // 2, lax.rem(bag, 2), sp // 4, lax.rem(sp, 4)
    row = lax.rem(y + 4 + sign * dy, 4)
    cores = [c, 1 - c]
    found = []
    for dx in range(4):
        bags = lax.rem(x + 4 + sign * dx, 4) * 2
        heads = lax.rem(z + 8 + sign * (g - dx - dy), 4) * 4 + row
        for dc in BOTH:
            found.append((dc, dc * 16 + dy * 4 + dx, (bags + cores[dc], heads)))
    return found


def each_row(g, sign, act, wanted):
    def one_row(dy, carry):
        act([(i, device) for dc, i, device in peers(g, dy, sign) if dc in wanted])
        return carry

    low = 0
    if g == 0:
        act([(i, device) for dc, i, device in peers(g, 0, sign) if dc in wanted and i])
        low = 1
    lax.fori_loop(low, 4, one_row, 0)


def norm(values):
    center = values - jnp.mean(values, axis=-1, keepdims=True)
    spread = jnp.mean(center * center, axis=-1, keepdims=True)
    return center * lax.rsqrt(spread + EPS)


def gelu(values):
    scale = -2.0 * math.sqrt(2.0 / math.pi) * math.log2(math.e)
    bent = values * (scale + (scale * 0.044715) * (values * values))
    return values / (1.0 + jnp.exp2(bent))


def two_mods(mod_ref, r, which):
    return jnp.concatenate(
        [
            jnp.broadcast_to(mod_ref[which, pl.ds(2 * r, 1), :], (CAP, D)),
            jnp.broadcast_to(mod_ref[which, pl.ds(2 * r + 1, 1), :], (CAP, D)),
        ],
        axis=0,
    )


def kernel(
    tok_ref, seq_ref, mod_ref, wqkv_hbm, wout_hbm, wfc1_hbm, wfc2_hbm, out_ref, place, safe_ref,
    wbig, wfc2, send, recv, kbuf, vbuf, qbuf, acc_s, stage, peak, wide, xs, norms, att, act, bound_ref,
    bias_s, osend, orecv, w_sem, ssem, rsem, ssem2, rsem2,
):
    bag, sp = lax.axis_index("bag"), lax.axis_index("sp")
    me = bag * H + sp
    barrier = pltpu.get_barrier_semaphore()

    copy_qkv = pltpu.make_async_copy(wqkv_hbm, wbig, w_sem.at[0])
    copy_qkv.start()
    copy_fc2 = pltpu.make_async_copy(wfc2_hbm, wfc2, w_sem.at[1])
    copy_fc2.start()

    def greet(device):
        pl.semaphore_signal(barrier, inc=1, device_id=device, device_id_type=MESH)

    for g in range(1, GROUPS):
        greet(peers(g, 0, 1)[0][2])

    seq = seq_ref[...]
    member = (lax.broadcasted_iota(jnp.int32, (BAGS, ROWS), 0) == seq).astype(F32)
    earlier = (
        lax.broadcasted_iota(jnp.int32, (ROWS, ROWS), 0)
        < lax.broadcasted_iota(jnp.int32, (ROWS, ROWS), 1)
    ).astype(BF16)
    before = jnp.dot(member.astype(BF16), earlier, preferred_element_type=F32)
    rank = jnp.sum(member * before, axis=0, keepdims=True)
    position = seq.astype(F32) * CAP + rank
    one_hot = (
        lax.broadcasted_iota(jnp.int32, (SLOTS, ROWS), 0).astype(F32) == position
    ).astype(F32)
    bias_s[...] = jnp.broadcast_to(
        (jnp.sum(one_hot, axis=1, keepdims=True) - 1.0) * BIG, (SLOTS, 128)
    )
    place[...] = one_hot.astype(BF16)
    xs[...] = jnp.dot(place[...], tok_ref[...], preferred_element_type=F32)

    @pl.loop(0, BAGS // 2)
    def _(r):
        for dy in range(4):
            for _, i, device in peers(r, dy, 1):
                if i:
                    greet(device)
        rows = pl.ds(pl.multiple_of(r * 2 * CAP, 2 * CAP), 2 * CAP)
        norms[rows, :] = (
            norm(xs[rows, :]) * (1.0 + two_mods(mod_ref, r, 1)) + two_mods(mod_ref, r, 0)
        ).astype(BF16)

    copy_qkv.wait()
    scale = math.log2(math.e) / math.sqrt(HD)
    for part in range(3):
        cols = pl.ds(part * D, D)
        wide[:, cols] = jnp.dot(norms[...], wbig[:, cols], preferred_element_type=F32) * (
            scale if part == 0 else 1.0
        )
    feature = lax.broadcasted_iota(jnp.int32, (2 * D, 128), 0)
    first = lax.broadcasted_iota(jnp.int32, (2 * D, 128), 1) * HD
    segment = ((feature >= first) & (feature < first + HD)).astype(BF16)
    squares = wide[:, 0 : 2 * D]
    lengths = 1.02 * jnp.dot(
        (squares * squares).astype(BF16), segment, preferred_element_type=F32
    )
    longest = jnp.max(lengths, axis=0, keepdims=True)
    lane1 = lax.broadcasted_iota(jnp.int32, (1, 128), 1)
    long_q = jnp.max(jnp.where(lane1 < H, longest, 0.0), axis=1, keepdims=True)
    long_k = jnp.max(jnp.where(lane1 >= H, longest, 0.0), axis=1, keepdims=True)
    peak[0:1, :] = jnp.where(lane1 == QLANE, long_q, jnp.where(lane1 == QLANE + 1, long_k, 0.0))
    copy_out = pltpu.make_async_copy(wout_hbm, wbig.at[:, pl.ds(0, D)], w_sem.at[2])
    copy_out.start()
    copy_fc1 = pltpu.make_async_copy(wfc1_hbm, wbig.at[:, pl.ds(D, FF)], w_sem.at[3])
    copy_fc1.start()

    lane = lax.broadcasted_iota(jnp.int32, (CAP, 128), 1)

    @pl.loop(0, BAGS)
    def _(r):
        rows = pl.ds(pl.multiple_of(r * CAP, 8), CAP)

        def piece(column, width, target):
            first, off = column // 128 * 128, column % 128
            shift = (target - off) % 128
            main = wide[rows, first : first + 128]
            if shift:
                main = pltpu.roll(main, shift, 1)
            if off + width > 128:
                rest = wide[rows, first + 128 : first + 256]
                if shift:
                    rest = pltpu.roll(rest, shift, 1)
                main = jnp.where(lane < target + 128 - off, main, rest)
            return main

        bias = bias_s[rows, :]
        lengths = jnp.broadcast_to(peak[0:1, :], (CAP, 128))
        for h in range(H):
            keys = jnp.where(lane < HD, piece(D + HD * h, HD, 0), piece(HD * h, QHEAD, HD + 1))
            keys = jnp.where(lane == HD, bias, keys)
            values = jnp.where(
                lane < HD,
                piece(2 * D + HD * h, HD, 0),
                piece(HD * h + QHEAD, HD - QHEAD, HD + 1),
            )
            values = jnp.where(lane == HD, 1.0, values)
            values = jnp.where(lane < HD + 1 + HD - QHEAD, values, lengths)
            send[r * H + h] = jnp.concatenate([keys, values], axis=0).astype(BF16)

    pl.semaphore_wait(barrier, DEVS - 1)
    def push_stage(stage):
        g, cores, _, _ = STAGES[stage]

        def push(row):
            for i, device in row:
                pltpu.make_async_remote_copy(
                    src_ref=send.at[device[0] * H + device[1]],
                    dst_ref=recv.at[g * PER + i],
                    send_sem=ssem.at[stage],
                    recv_sem=rsem.at[stage],
                    device_id=device,
                    device_id_type=MESH,
                ).start()

        each_row(g, 1, push, cores)

    push_stage(0)
    push_stage(1)
    push_stage(2)
    push_stage(3)
    recv[0] = send[me]

    def stage_copy(stage):
        _, _, first, count = STAGES[stage]
        skip = 1 if stage == 0 else 0
        block = recv.at[pl.ds(first + skip, count - skip)]
        return pltpu.make_async_remote_copy(
            src_ref=block,
            dst_ref=block,
            send_sem=ssem.at[stage],
            recv_sem=rsem.at[stage],
            device_id=(bag, lax.rem(sp + 1, H)),
            device_id_type=MESH,
        )

    lane2 = lax.broadcasted_iota(jnp.int32, (2 * CAP, 128), 1)

    def unpack(source, count):
        def two(n, top):
            one = recv[2 * n].astype(F32)
            two = recv[2 * n + 1].astype(F32)
            keys = jnp.concatenate([one[:CAP], two[:CAP]], axis=0)
            values = jnp.concatenate([one[CAP:], two[CAP:]], axis=0)
            query = jnp.where(
                lane2 < QHEAD,
                pltpu.roll(keys, 127 - HD, 1),
                pltpu.roll(values, (QHEAD - HD - 1) % 128, 1),
            )
            query = jnp.where(lane2 < HD, query, jnp.where(lane2 == HD, 1.0, 0.0))
            rows = pl.ds(pl.multiple_of(n * 2 * CAP, 2 * CAP), 2 * CAP)
            kbuf[rows, :] = keys.astype(BF16)
            qbuf[rows, :] = query.astype(BF16)
            near = pl.ds(pl.multiple_of((n - source // 2) * 2 * CAP, 2 * CAP), 2 * CAP)
            stage[near, :] = values
            return jnp.maximum(top, values)

        top = lax.fori_loop(
            source // 2, (source + count) // 2, two, jnp.zeros((2 * CAP, 128), F32), unroll=8
        )
        bound_ref[...] = jnp.maximum(
            bound_ref[...], jnp.broadcast_to(jnp.max(top, axis=0, keepdims=True), (8, 128))
        )
        vbuf[:, source * CAP : (source + count) * CAP] = (
            stage[0 : count * CAP, :].T[0:WIDE].astype(BF16)
        )

    def attend(first, rows, key_first, key_rows):
        keys = pl.ds(key_first, key_rows)
        queries = slice(first, first + rows)
        scores = lax.dot_general(
            kbuf[keys, :], qbuf[queries, :], (((1,), (1,)), ((), ())), preferred_element_type=F32
        )
        acc_s[:, queries] += jnp.dot(
            vbuf[:, keys], jnp.exp2(scores).astype(BF16), preferred_element_type=F32
        )

    lane32 = lax.broadcasted_iota(jnp.int32, (8, 128), 1)

    def give_back(stage_of):
        g, cores, source, count = STAGES[stage_of]
        mixed = acc_s[:, source * CAP : (source + count) * CAP]
        mixed = mixed * (1.0 / mixed[HD : HD + 1, :])
        stage[0 : count * CAP, :] = jnp.concatenate(
            [mixed, jnp.zeros((128 - WIDE, count * CAP), F32)], axis=0
        ).T

        def packed(i):
            near = pl.multiple_of((g * PER + i - source) * CAP, 8)
            mixed = stage[pl.ds(near, CAP), :]
            tail = mixed[32:40]
            return jnp.concatenate(
                [
                    jnp.where(lane32 < HD, mixed[0:8], pltpu.roll(tail, HD, 1)),
                    jnp.where(lane32 < HD, mixed[8:16], pltpu.roll(tail, 16, 1)),
                    mixed[16:32],
                ],
                axis=0,
            ).astype(BF16)

        def push(row):
            for i, _ in row:
                osend[g * PER + i] = packed(i)
            for i, device in row:
                pltpu.make_async_remote_copy(
                    src_ref=osend.at[g * PER + i],
                    dst_ref=orecv.at[me],
                    send_sem=ssem2,
                    recv_sem=rsem2,
                    device_id=device,
                    device_id_type=MESH,
                ).start()

        each_row(g, -1, push, cores)
        if stage_of == 0:
            orecv[me] = packed(0)

    acc_s[...] = jnp.zeros((WIDE, KEYS), F32)
    bound_ref[...] = jnp.zeros((8, 128), F32)
    for n, (_, _, source, count) in enumerate(STAGES):
        stage_copy(n).wait_recv()
        unpack(source, count)
        last = n == len(STAGES) - 1
        for t in range(n):
            attend(STAGES[t][2] * CAP, STAGES[t][3] * CAP, source * CAP, count * CAP)
            if last:
                give_back(t)
        whole = (source + count) // PER

        @pl.loop(0, whole)
        def _(k, source=source, count=count):
            attend(source * CAP, count * CAP, pl.multiple_of(k * GROWS, GROWS), GROWS)

        if whole * PER < source + count:
            attend(source * CAP, count * CAP, source * CAP, count * CAP)
        if last:
            give_back(n)

    def return_copy(buf, lo):
        block = buf.at[pl.ds(lo, DEVS - 1)]
        return pltpu.make_async_remote_copy(
            src_ref=block,
            dst_ref=block,
            send_sem=ssem2,
            recv_sem=rsem2,
            device_id=(bag, lax.rem(sp + 1, H)),
            device_id_type=MESH,
        )

    return_copy(orecv, 0).wait_recv()

    @pl.loop(0, BAGS // 2)
    def _(rp):
        halves = []
        for r in range(2):
            moved = []
            for h in range(H):
                block = orecv[(2 * rp + r) * H + h].astype(F32)
                tail = jnp.where(
                    lane32 < 128 - HD,
                    pltpu.roll(block[0:8], 128 - HD, 1),
                    pltpu.roll(block[8:16], 112, 1),
                )
                whole = jnp.concatenate([block, tail], axis=0)
                shift = HD * h % 128
                moved.append(pltpu.roll(whole, shift, 1) if shift else whole)
            columns = []
            for j in range(D // 128):
                first = 128 * j // HD
                column = moved[first]
                for h in range(first + 1, H):
                    if HD * h >= 128 * (j + 1):
                        break
                    column = jnp.where(lane < HD * h - 128 * j, column, moved[h])
                columns.append(column)
            halves.append(columns)
        rows = pl.ds(pl.multiple_of(rp * 2 * CAP, 2 * CAP), 2 * CAP)
        for j in range(D // 128):
            att[rows, 128 * j : 128 * j + 128] = jnp.concatenate(
                [halves[0][j], halves[1][j]], axis=0
            ).astype(BF16)

    copy_out.wait()
    wide[:, 0:D] = jnp.dot(att[...], wbig[:, 0:D], preferred_element_type=F32)

    @pl.loop(0, BAGS // 2, unroll=True)
    def _(r):
        rows = pl.ds(pl.multiple_of(r * 2 * CAP, 2 * CAP), 2 * CAP)
        hidden = (xs[rows, :] + two_mods(mod_ref, r, 2) * wide[rows, 0:D]).astype(BF16).astype(F32)
        xs[rows, :] = hidden
        norms[rows, :] = (
            norm(hidden) * (1.0 + two_mods(mod_ref, r, 4)) + two_mods(mod_ref, r, 3)
        ).astype(BF16)

    copy_fc1.wait()
    copy_fc2.wait()
    width = FF // 3

    def inner(part):
        first = D + width * part
        return jnp.dot(
            norms[...], wbig[:, first : first + width], preferred_element_type=F32
        )

    now = inner(0)
    for part in range(3):
        later = inner(part + 1) if part < 2 else None
        act[:, width * part : width * (part + 1)] = gelu(now).astype(BF16)
        now = later
    wide[:, 0:D] = jnp.dot(act[...], wfc2[...], preferred_element_type=F32)

    @pl.loop(0, BAGS // 2, unroll=True)
    def _(r):
        rows = pl.ds(pl.multiple_of(r * 2 * CAP, 2 * CAP), 2 * CAP)
        out_ref[rows, :] = (xs[rows, :] + two_mods(mod_ref, r, 5) * wide[rows, 0:D]).astype(BF16)

    top = bound_ref[0:1, :]
    long_q = jnp.max(jnp.where(lane1 == QLANE, top, 0.0))
    long_k = jnp.max(jnp.where(lane1 == QLANE + 1, top, 0.0))
    safe_ref[0, 0] = (long_q * long_k < LIMIT * LIMIT).astype(jnp.int32)

    for n in range(len(STAGES)):
        stage_copy(n).wait_send()
    return_copy(osend, 1).wait_send()


def fused(tokens, row_seq, modulation, w_qkv, w_out, w_fc1, w_fc2):
    vmem = pl.BlockSpec(memory_space=pltpu.VMEM)
    anywhere = pl.BlockSpec(memory_space=pl.ANY)
    return pl.pallas_call(
        kernel,
        out_shape=[
            jax.ShapeDtypeStruct((SLOTS, D), BF16),
            jax.ShapeDtypeStruct((SLOTS, ROWS), BF16),
            jax.ShapeDtypeStruct((1, 1), jnp.int32),
        ],
        in_specs=[vmem, vmem, vmem, anywhere, anywhere, anywhere, anywhere],
        out_specs=[vmem, vmem, pl.BlockSpec(memory_space=pltpu.SMEM)],
        scratch_shapes=[
            pltpu.VMEM((D, 3 * D), BF16),
            pltpu.VMEM((FF, D), BF16),
            pltpu.VMEM((DEVS, 2 * CAP, 128), BF16),
            pltpu.VMEM((DEVS, 2 * CAP, 128), BF16),
            pltpu.VMEM((KEYS, 128), BF16),
            pltpu.VMEM((WIDE, KEYS), BF16),
            pltpu.VMEM((KEYS, 128), BF16),
            pltpu.VMEM((WIDE, KEYS), F32),
            pltpu.VMEM((GROWS, 128), F32),
            pltpu.VMEM((8, 128), F32),
            pltpu.VMEM((SLOTS, 3 * D), F32),
            pltpu.VMEM((SLOTS, D), F32),
            pltpu.VMEM((SLOTS, D), BF16),
            pltpu.VMEM((SLOTS, D), BF16),
            pltpu.VMEM((SLOTS, FF), BF16),
            pltpu.VMEM((8, 128), F32),
            pltpu.VMEM((SLOTS, 128), F32),
            pltpu.VMEM((DEVS, 32, 128), BF16),
            pltpu.VMEM((DEVS, 32, 128), BF16),
            pltpu.SemaphoreType.DMA((4,)),
            pltpu.SemaphoreType.DMA((len(STAGES),)),
            pltpu.SemaphoreType.DMA((len(STAGES),)),
            pltpu.SemaphoreType.DMA,
            pltpu.SemaphoreType.DMA,
        ],
        compiler_params=pltpu.CompilerParams(
            collective_id=0, has_side_effects=True, vmem_limit_bytes=62 * 2**20
        ),
    )(tokens, row_seq.reshape(1, ROWS), jnp.swapaxes(modulation, 0, 1), w_qkv, w_out, w_fc1, w_fc2)


def layer_norm(values):
    center = values - jnp.mean(values, axis=-1, keepdims=True)
    spread = jnp.mean(center * center, axis=-1, keepdims=True)
    return center * lax.rsqrt(spread + EPS)


def lookup(seq_codes, modulation):
    seq_total = modulation.shape[0]
    one_hot = (seq_codes[:, None] == jnp.arange(seq_total, dtype=jnp.int32)[None, :]).astype(
        jnp.float32
    )
    table_rows = modulation.reshape(seq_total, -1)
    picked = jnp.dot(
        one_hot, table_rows, precision=lax.Precision.HIGHEST, preferred_element_type=jnp.float32
    )
    return picked.reshape(seq_codes.shape[0], 6, -1)


def project(source_rows, mods, w_qkv):
    normed = (layer_norm(source_rows.astype(jnp.float32)) * (1.0 + mods[:, 1]) + mods[:, 0]).astype(
        jnp.bfloat16
    )
    return jnp.dot(normed, w_qkv, preferred_element_type=jnp.float32).astype(jnp.bfloat16)


def attend(packed, seq_codes):
    key_count = packed.shape[0]
    local_width = packed.shape[2]
    head_local = local_width // HD
    queries = packed[:, 0].reshape(key_count, head_local, HD)
    key_rows = packed[:, 1].reshape(key_count, head_local, HD)
    values = packed[:, 2].reshape(key_count, head_local, HD)
    block_size = math.gcd(key_count, 512)
    score_scale = 1.0 / math.sqrt(HD)

    def one_block(block_index):
        first_row = block_index * block_size
        query_part = lax.dynamic_slice_in_dim(queries, first_row, block_size, 0)
        query_seq = lax.dynamic_slice_in_dim(seq_codes, first_row, block_size, 0)
        scores = (
            jnp.einsum("qhd,khd->hqk", query_part, key_rows, preferred_element_type=jnp.float32)
            * score_scale
        )
        allowed = query_seq[:, None] == seq_codes[None, :]
        scores = jnp.where(allowed[None], scores, -jnp.inf)
        row_max = jnp.max(scores, axis=-1, keepdims=True)
        raised = jnp.exp(scores - row_max)
        denominator = jnp.sum(raised, axis=-1)
        probs = raised.astype(jnp.bfloat16)
        mixed_rows = jnp.einsum("hqk,khd->qhd", probs, values, preferred_element_type=jnp.float32)
        mixed_rows = mixed_rows / jnp.transpose(denominator)[:, :, None]
        return mixed_rows.astype(jnp.bfloat16).reshape(block_size, local_width)

    blocks = lax.map(one_block, jnp.arange(key_count // block_size, dtype=jnp.int32))
    return blocks.reshape(key_count, local_width)


def finish(residual, attended, mods, w_out, w_fc1, w_fc2):
    branch = jnp.dot(attended, w_out, preferred_element_type=jnp.float32)
    hidden = (residual.astype(jnp.float32) + mods[:, 2] * branch).astype(jnp.bfloat16)
    normed = (layer_norm(hidden.astype(jnp.float32)) * (1.0 + mods[:, 4]) + mods[:, 3]).astype(
        jnp.bfloat16
    )
    active = jax.nn.gelu(
        jnp.dot(normed, w_fc1, preferred_element_type=jnp.float32), approximate=True
    ).astype(jnp.bfloat16)
    return (
        hidden.astype(jnp.float32)
        + mods[:, 5] * jnp.dot(active, w_fc2, preferred_element_type=jnp.float32)
    ).astype(jnp.bfloat16)


def plan_with_maximum(tokens, row_seq, modulation, w_qkv, w_out, w_fc1, w_fc2):
    bag_count = lax.axis_size("bag")
    sp_count = lax.axis_size("sp")
    row_count, model_width = tokens.shape
    capacity = row_count // bag_count * 5 // 4
    slot_count = bag_count * capacity
    local_width = model_width // sp_count
    key_count = sp_count * slot_count
    bag_of = row_seq
    member = (bag_of[:, None] == jnp.arange(bag_count, dtype=jnp.int32)[None, :]).astype(jnp.int32)
    before = jnp.cumsum(member, axis=0) - member
    rank_in = jnp.sum(before * member, axis=1)
    position = bag_of * capacity + rank_in
    source_row = (
        jnp.zeros((slot_count,), jnp.int32).at[position].set(jnp.arange(row_count, dtype=jnp.int32))
    )
    filled = jnp.zeros((slot_count,), jnp.bool_).at[position].set(True)
    slot_seq = jnp.where(filled, jnp.take(row_seq, source_row), -1)
    send_rows = jnp.where(
        filled[:, None], jnp.take(tokens, source_row, axis=0), jnp.zeros((), jnp.bfloat16)
    )
    arrived, arrived_seq = (
        lax.all_to_all(send_rows, "bag", split_axis=0, concat_axis=0, tiled=True),
        lax.all_to_all(
            slot_seq.astype(jnp.bfloat16), "bag", split_axis=0, concat_axis=0, tiled=True
        ),
    )
    mods = lookup(arrived_seq.astype(jnp.int32), modulation)
    packed = project(arrived, mods, w_qkv).reshape(slot_count, 3, sp_count, local_width)
    code_copies = jnp.broadcast_to(arrived_seq[:, None, None, None], (slot_count, 1, sp_count, 1))
    by_head, head_seq = (
        lax.all_to_all(packed, "sp", split_axis=2, concat_axis=0, tiled=True),
        lax.all_to_all(code_copies, "sp", split_axis=2, concat_axis=0, tiled=True),
    )
    attended = attend(
        by_head.reshape(key_count, 3, local_width), head_seq.reshape(key_count).astype(jnp.int32)
    )
    by_slot = lax.all_to_all(
        attended.reshape(key_count, 1, local_width), "sp", split_axis=0, concat_axis=1, tiled=True
    )
    finished = finish(arrived, by_slot.reshape(slot_count, model_width), mods, w_out, w_fc1, w_fc2)
    returned = lax.all_to_all(finished, "bag", split_axis=0, concat_axis=0, tiled=True)
    return jnp.take(returned, position, axis=0)


def in_row_order(slots, place, *_):
    return lax.dot_general(
        place, slots, (((0,), (0,)), ((), ())), preferred_element_type=jnp.float32
    ).astype(jnp.bfloat16)


def shards(*operands):
    slots, place, safe = fused(*operands)
    return lax.cond(
        safe[0, 0] == 1,
        in_row_order,
        lambda slots, place, *rest: plan_with_maximum(*rest),
        slots,
        place,
        *operands,
    )


def solution(mesh):
    placed = (P(("bag", "sp"), None), P(("bag", "sp")), P(), P(), P(), P(), P())
    return jax.shard_map(
        shards, mesh=mesh, in_specs=placed, out_specs=P(("bag", "sp"), None), check_vma=False
    )
```
